768 devices in a mesh: batch: 48 (over x, z), segment: 2 (over y_lo), seq: 8 (over y_hi, core).
Axes of the slice: x: 4, y: 8 (y_hi: 4, y_lo: 2; y = y_hi * 2 + y_lo), z: 12, core: 2. Of those that a mesh axis runs over, the one named last changes fastest.
Arguments:
- dna_features: bfloat16 [48, 2, 1536, 768], P('batch', None, 'seq'), may hold values from -6 to 6
- depth_weight: bfloat16 [3, 768], replicated, may hold values from -3.5 to 3.5
- point_weight: bfloat16 [768, 1536], replicated, may hold values from -0.21875 to 0.21875
- query_weight: bfloat16 [1536, 512], replicated, may hold values from -0.15625 to 0.15625
- key_weight: bfloat16 [1536, 128], replicated, may hold values from -0.15625 to 0.15625
- value_weight: bfloat16 [1536, 192], replicated, may hold values from -0.15625 to 0.15625
- cotangent: bfloat16 [48, 2, 768, 768], P('batch', None, 'seq'), may hold values from -6 to 6
Outputs:
- encoded: bfloat16 [48, 2, 768, 1536], P('batch', None, 'seq')
- grad_output: float32 [768, 768], P(('batch', 'segment', 'seq'))
The draws below stay inside these ranges and needn't reach their ends.
All inputs are finite; a program needn't handle non-finite values.
Results may differ from the reference program's by a relative error of at most 0.005.
Values may be sent and summed in bfloat16 or wider, within the bound.
A program may use at most 32 MiB of HBM per device.

```python
import math
import jax
import jax.numpy as jnp
from jax import lax

C_IN = 768
D = 1536
GRAD_ROWS = 768
HEADS = 4
KEY_DIM = 128
VALUE_DIM = 192
MICRO = 2
WINDOWS = 48
LENGTH = 768
LENGTH_IN = 1536
QUERY_W = 512


def strengthened(entries, stream_key, source, target, blocks, factor):
    def block_of(dim):
        return (jnp.arange(entries.shape[dim]) // (entries.shape[dim] // blocks)).reshape((-1,) + (1,) * (entries.ndim - 1 - dim))

    one_side = jax.random.permutation(stream_key, blocks)[block_of(target)]
    other_side = (block_of(target) + blocks // 2) % blocks
    return jnp.where((block_of(source) == one_side) | (block_of(source) == other_side), factor * entries, entries)


def shard_levels(rng, dims, cuts, least, top_value):
    factor_of, own = 1.0, jax.random.fold_in(rng, 6)
    for position, shards_of in cuts:
        heights = jnp.exp(jax.random.uniform(jax.random.fold_in(own, position), (shards_of,), jnp.float32, least / len(cuts), top_value / len(cuts)))
        factor_of = factor_of * jnp.repeat(heights, dims[position] // shards_of).reshape([-1 if axis == position else 1 for axis in range(len(dims))])
    return factor_of


def noise(stream_key, shape, deviation, limit, pieces=(), dtype=jnp.bfloat16):
    array = jax.random.normal(stream_key, shape, jnp.float32) * deviation
    if len(pieces) > 0:
        array = shard_levels(stream_key, shape, pieces, -0.22, 0.18) * array
    return jnp.clip(array, min=-limit, max=limit).astype(dtype)


def heavy_noise(stream_key, extent, deviation, reach, shards, heavy, held_as=jnp.bfloat16):
    array = deviation * jax.random.normal(stream_key, extent, jnp.float32)
    if shards:
        array = array * shard_levels(stream_key, extent, shards, -0.22, 0.18)
    return jnp.clip(strengthened(array, jax.random.fold_in(stream_key, 3), *heavy), -reach, reach).astype(held_as)


def setup_inputs(seed: int = 0) -> dict:
    arg_keys = jax.random.split(jax.random.key(seed), 8)
    return {
        "dna_features": noise(arg_keys[0], (WINDOWS, MICRO, LENGTH_IN, C_IN), 1.0, 6.0, ((0, 48), (2, 8))),
        "depth_weight": noise(arg_keys[1], (3, C_IN), 3 ** -0.5, 3.5),
        "point_weight": noise(arg_keys[2], (C_IN, D), C_IN ** -0.5, 0.21875),
        "query_weight": noise(arg_keys[3], (D, QUERY_W), D ** -0.5, 0.15625),
        "key_weight": noise(arg_keys[4], (D, KEY_DIM), D ** -0.5, 0.15625),
        "value_weight": noise(arg_keys[5], (D, VALUE_DIM), D ** -0.5, 0.15625),
        "cotangent": heavy_noise(arg_keys[6], (WINDOWS, MICRO, LENGTH, GRAD_ROWS), 1.0, 6.0, ((0, 48), (2, 8)), (0, 3, 48, 3.25)),
    }


EPSILON = 1e-06

def rms_scale(values):
    return values * lax.rsqrt(lax.optimization_barrier(jnp.mean(values * values, axis=-1, keepdims=True)) + EPSILON)

def one_window(features, depth_weight, point_weight, query_weight, key_weight, value_weight):
    micro = features.shape[0]
    length_in = features.shape[1]
    channels = features.shape[2]
    length = length_in // 2
    padded = jnp.pad(features, ((0, 0), (2, 2), (0, 0))).astype(jnp.float32)
    summed = jnp.zeros((micro, length, channels), jnp.float32)
    for tap in range(3):
        summed = summed + depth_weight[tap].astype(jnp.float32) * padded[:, 2 * tap:2 * tap + length_in:2, :]
    pooled = summed.astype(jnp.bfloat16).reshape(micro * length, channels)
    encoded = jax.nn.gelu(jnp.dot(pooled, point_weight, preferred_element_type=jnp.float32)).astype(jnp.bfloat16)
    normed = rms_scale(encoded.astype(jnp.float32)).astype(jnp.bfloat16)
    queries = jnp.dot(normed, query_weight, preferred_element_type=jnp.float32).reshape(micro, length, HEADS, KEY_DIM)
    queries = rms_scale(queries).astype(jnp.bfloat16)
    key_rows = rms_scale(jnp.dot(normed, key_weight, preferred_element_type=jnp.float32)).astype(jnp.bfloat16)
    key_rows = key_rows.reshape(micro, length, KEY_DIM)
    value_rows = jnp.dot(normed, value_weight, preferred_element_type=jnp.float32).astype(jnp.bfloat16)
    value_rows = value_rows.reshape(micro, length, VALUE_DIM)
    scores = jnp.einsum('mrhd,mpd->mhrp', queries.astype(jnp.float32), key_rows.astype(jnp.float32))
    scores = scores * (1.0 / math.sqrt(KEY_DIM))
    weights = jnp.exp(scores)
    denominator = lax.optimization_barrier(jnp.sum(weights, axis=-1))
    rounded = lax.optimization_barrier(weights.astype(jnp.bfloat16))
    numerator = jnp.einsum('mhrp,mpe->mrhe', rounded.astype(jnp.float32), value_rows.astype(jnp.float32))
    attended = numerator / jnp.transpose(denominator, (0, 2, 1))[..., None]
    attended = attended.astype(jnp.bfloat16).reshape(micro, length, HEADS * VALUE_DIM)
    return (encoded.reshape(micro, length, point_weight.shape[1]), attended)

def reference(dna_features, depth_weight, point_weight, query_weight, key_weight, value_weight, cotangent):

    def per_window(features):
        return one_window(features, depth_weight, point_weight, query_weight, key_weight, value_weight)
    encoded, attended = lax.map(per_window, dna_features)
    windows = encoded.shape[0]
    micro = encoded.shape[1]
    all_rows = windows * micro * encoded.shape[2]
    grad_width = cotangent.shape[3]
    flat_cotangent = cotangent.reshape(all_rows, grad_width)
    flat_attended = attended.reshape(all_rows, attended.shape[3])
    grad_output = jnp.dot(flat_cotangent.T, flat_attended, preferred_element_type=jnp.float32)
    grad_output = grad_output * (1.0 / math.sqrt(windows * micro))
    return (encoded, grad_output)
```

```python
import functools
import math

import jax
import jax.numpy as jnp
from jax import lax
from jax.experimental import pallas as pl
from jax.experimental.pallas import tpu as pltpu
from jax.sharding import PartitionSpec as P

MESH = pl.DeviceIdType.MESH
F32 = jnp.float32
BF16 = jnp.bfloat16

C_IN = 768
D = 1536
KEY = 128
VAL = 192
ROWS = 96
X, Z, S = 4, 12, 8
EPSILON = 1e-06
LANE = 128
COL = 256
KV_W = 384
EXP2_SCALE = math.log2(math.e) / math.sqrt(KEY)


def gelu(u):
    inner = math.sqrt(2.0 / math.pi) * (u + 0.044715 * (u * u * u))
    return 0.5 * u * (1.0 + jnp.tanh(inner))


def rms_of(values):
    return lax.rsqrt(jnp.mean(values * values, axis=-1, keepdims=True) + EPSILON)


def kernel(
    norm,
    dna, dw, pw, qw, kw, vw, cot,
    enc_out, grad_out,
    xin, dwv, pwv, qwv, kwv, vwv, cotv,
    xf, ext, pooled, enc, ssq, rinv, qacc, kacc, vacc,
    hs, hr, q4, qall, kvs, kvbuf, acc, cott, att2, psend, p1r, red1, p2s, p2r, p3s, p3r,
    in_sem, enc_sem, h_send, h_recv, cot_send, cot_recv, q_send, q_recv,
    d_send, d_recv, r_send, r_recv, p1_send, p1_recv, p2_send, p2_recv, p3_send, p3_recv,
):
    b, g, s = lax.axis_index("batch"), lax.axis_index("segment"), lax.axis_index("seq")
    x, z = b // Z, lax.rem(b, Z)
    h, c = s // 2, lax.rem(s, 2)
    other = 1 - g
    sign = 2 * g - 1
    sib = (b, g, h * 2 + (1 - c))

    def gx_peer(dx, dg):
        return (lax.rem(x + dx, X) * Z + z, lax.rem(g + dg, 2), s)

    def s_peer(d):
        return (b, g, lax.rem(s + d, S))

    def z_peer(d):
        return (x * Z + lax.rem(z + d, Z), g, s)

    near = (b, other, lax.rem(h + sign + 4, 4) * 2 + c)
    middle = (b, g, lax.rem(h + sign + 4, 4) * 2 + c)
    far = (b, other, lax.rem(h + 2, 4) * 2 + c)

    loads = [
        pltpu.make_async_copy(dna.at[0], xin, in_sem.at[0]),
        pltpu.make_async_copy(dw, dwv, in_sem.at[1]),
        pltpu.make_async_copy(cot.at[0, g], cotv.at[0], in_sem.at[2]),
        pltpu.make_async_copy(pw, pwv, in_sem.at[3]),
        pltpu.make_async_copy(kw, kwv, in_sem.at[4]),
        pltpu.make_async_copy(vw, vwv, in_sem.at[5]),
        pltpu.make_async_copy(qw, qwv, in_sem.at[6]),
    ]
    for load in loads:
        load.start()

    barrier = pltpu.get_barrier_semaphore()

    def hello(device):
        pl.semaphore_signal(barrier, inc=1, device_id=device, device_id_type=MESH)

    for d in range(1, Z):
        hello(z_peer(d))
    for d in range(1, 8):
        hello(gx_peer(d // 2, d % 2))
    for d in range(1, S):
        hello(s_peer(d))
    hello(near)
    hello(far)

    loads[0].wait()
    for m in range(2):
        for k in range(6):
            i = m * 6 + k
            xf[k] = xin[m, :, k * LANE : (k + 1) * LANE].astype(F32)
            even = xf[k, pl.ds(0, ROWS, stride=2), :]
            ext[i, 8 : 8 + ROWS, :] = even
            hs[0, i] = even[0:1]
            hs[1, i] = even[ROWS - 1 : ROWS]
    lane = lax.broadcasted_iota(jnp.int32, (ROWS, LANE), 1)
    ones = jnp.where(lane >= VAL - LANE, 1.0, 0.0).astype(BF16)
    for m in range(2):
        kvs[m, :, 2 * LANE : 3 * LANE] = ones
    loads[1].wait()
    loads[2].wait()

    pl.semaphore_wait(barrier, 11 + 7 + 7 + 2)

    to_left = pltpu.make_async_remote_copy(
        src_ref=hs.at[0], dst_ref=hr.at[1], send_sem=h_send.at[0], recv_sem=h_recv.at[1],
        device_id=s_peer(S - 1), device_id_type=MESH,
    )
    to_right = pltpu.make_async_remote_copy(
        src_ref=hs.at[1], dst_ref=hr.at[0], send_sem=h_send.at[1], recv_sem=h_recv.at[0],
        device_id=s_peer(1), device_id_type=MESH,
    )
    to_left.start()
    to_right.start()
    cot_copy = pltpu.make_async_remote_copy(
        src_ref=cotv.at[0], dst_ref=cotv.at[1], send_sem=cot_send, recv_sem=cot_recv,
        device_id=sib, device_id_type=MESH,
    )
    cot_copy.start()
    to_left.wait()
    to_right.wait()

    w = dwv[...].astype(F32)
    for m in range(2):
        for k in range(6):
            i = m * 6 + k
            ext[i, 7:8, :] = jnp.where(s > 0, hr[0, i], 0.0)
            ext[i, 8 + ROWS : 9 + ROWS, :] = jnp.where(s < S - 1, hr[1, i], 0.0)
            part = slice(k * LANE, (k + 1) * LANE)
            total = w[0:1, part] * ext[i, 7 : 7 + ROWS, :]
            total = total + w[1:2, part] * ext[i, 8 : 8 + ROWS, :]
            total = total + w[2:3, part] * ext[i, 9 : 9 + ROWS, :]
            pooled[m * ROWS : (m + 1) * ROWS, part] = total.astype(BF16)

    for load in loads[3:]:
        load.wait()
    ssq[...] = jnp.zeros_like(ssq)
    qacc[...] = jnp.zeros_like(qacc)
    kacc[...] = jnp.zeros_like(kacc)
    vacc[...] = jnp.zeros_like(vacc)

    def encode(n, _):
        cols = pl.ds(pl.multiple_of(n * COL, COL), COL)
        u = jnp.dot(pooled[...], pwv[:, cols], preferred_element_type=F32)
        rows = gelu(u).astype(BF16)
        enc[n] = rows.reshape(2, ROWS, COL)
        wide = rows.astype(F32)
        square = wide * wide
        ssq[...] += square[:, :LANE] + square[:, LANE:]
        kacc[...] += jnp.dot(rows, kwv[cols, :], preferred_element_type=F32)
        vacc[...] += jnp.dot(rows, vwv[cols, :], preferred_element_type=F32)
        qacc[...] += jnp.dot(enc[n, g], qwv[cols, :], preferred_element_type=F32)
        pltpu.make_async_copy(enc.at[n], enc_out.at[0, :, :, cols], enc_sem.at[n]).start()
        return 0

    lax.fori_loop(0, D // COL, encode, 0)

    scale = lax.rsqrt(jnp.sum(ssq[...], axis=-1, keepdims=True) * (1.0 / D) + EPSILON)
    rinv[...] = jnp.broadcast_to(scale, (2 * ROWS, LANE)).reshape(2, ROWS, LANE)
    keys = kacc[...] * scale
    keys = (keys * rms_of(keys)).astype(BF16)
    values = (vacc[...] * scale).astype(BF16)
    for m in range(2):
        kvs[m, :, :KEY] = keys[m * ROWS : (m + 1) * ROWS]
        kvs[m, :, KEY : KEY + VAL] = values[m * ROWS : (m + 1) * ROWS]

    def kv_copy(j, block, slot, device):
        return pltpu.make_async_remote_copy(
            src_ref=kvs.at[block], dst_ref=kvbuf.at[slot], send_sem=d_send.at[j],
            recv_sem=d_recv.at[j], device_id=device, device_id_type=MESH,
        )

    def relay(j, source):
        return pltpu.make_async_remote_copy(
            src_ref=source, dst_ref=kvbuf.at[2 * j + 1], send_sem=r_send.at[j],
            recv_sem=r_recv.at[j], device_id=sib, device_id_type=MESH,
        )

    direct = [kv_copy(0, other, 2, near), kv_copy(1, g, 4, middle), kv_copy(2, other, 6, far)]
    for copy in direct:
        copy.start()
    relays = [relay(0, kvs.at[g])]
    relays[0].start()
    kvbuf[0] = kvs[g]

    row_scale = rinv[g]
    for i in range(4):
        query = qacc[:, i * KEY : (i + 1) * KEY] * row_scale
        q4[i] = (query * rms_of(query)).astype(BF16)
    q_copy = pltpu.make_async_remote_copy(
        src_ref=q4.at[pl.ds(2 * (1 - c), 2)], dst_ref=qall.at[:, 1], send_sem=q_send,
        recv_sem=q_recv, device_id=sib, device_id_type=MESH,
    )
    q_copy.start()
    qall[:, 0] = q4[pl.ds(2 * c, 2)]

    cot_copy.wait()
    turned = jnp.transpose(cotv[...].reshape(2 * ROWS, C_IN))
    cott[...] = turned.reshape(X, 2 * ROWS, 2 * ROWS)

    def attend(j):
        block = kvbuf[2 * j : 2 * j + 2].reshape(2 * ROWS, KV_W)
        query = qall[...].reshape(4 * ROWS, KEY)
        scores = lax.dot_general(
            query, block[:, :KEY], (((1,), (1,)), ((), ())), preferred_element_type=F32
        )
        weights = jnp.exp2(scores * EXP2_SCALE).astype(BF16)
        part = jnp.dot(weights, block[:, KEY:], preferred_element_type=F32)
        if j == 0:
            acc[...] = part
        else:
            acc[...] += part

    def pass_on(j):
        direct[j - 1].wait_recv()
        relays.append(relay(j, kvbuf.at[2 * j]))
        relays[j].start()

    q_copy.wait_recv()
    relays[0].wait_recv()
    attend(0)
    pass_on(1)
    pass_on(2)
    relays[1].wait_recv()
    attend(1)
    pass_on(3)
    relays[2].wait_recv()
    attend(2)
    relays[3].wait_recv()
    attend(3)

    total = acc[...]
    attended = (total[:, :VAL] / total[:, VAL : VAL + 1]).astype(BF16)
    att2[...] = jnp.concatenate([attended[: 2 * ROWS], attended[2 * ROWS :]], axis=1)

    def p1_copy(dx, dg):
        i = dx * 2 + dg
        return pltpu.make_async_remote_copy(
            src_ref=psend.at[i], dst_ref=p1r.at[i], send_sem=p1_send.at[i],
            recv_sem=p1_recv.at[i], device_id=gx_peer(dx, dg), device_id_type=MESH,
        )

    for dx in (2, 1, 3, 0):
        share = jnp.dot(cott[lax.rem(x + dx, X)], att2[...], preferred_element_type=F32)
        share = share.reshape(Z, 2, S, 2 * VAL)
        low, high = share[:, 0].reshape(Z * S, 2 * VAL), share[:, 1].reshape(Z * S, 2 * VAL)
        same, cross = jnp.where(g == 0, low, high), jnp.where(g == 0, high, low)
        psend[dx * 2 + 1] = cross.astype(BF16)
        p1_copy(dx, 1).start()
        psend[dx * 2] = same.astype(BF16)
        if dx > 0:
            p1_copy(dx, 0).start()
    total = psend[0].astype(F32)
    for i in (1, 2, 3, 6, 7, 4, 5):
        p1_copy(i // 2, i % 2).wait_recv()
        total = total + p1r[i].astype(F32)

    for k in range(3):
        red1[k, : Z * S, :] = total[:, k * LANE : (k + 1) * LANE]
        red1[k, Z * S :, :] = jnp.zeros((S * 16 - Z * S, LANE), F32)
    for i in range(S):
        for k in range(3):
            p2s[i, :, k * LANE : (k + 1) * LANE] = red1[k, pl.ds(i, 16, stride=S), :].astype(BF16)

    def p2_copy(d):
        return pltpu.make_async_remote_copy(
            src_ref=p2s.at[lax.rem(s + d, S)], dst_ref=p2r.at[d], send_sem=p2_send.at[d],
            recv_sem=p2_recv.at[d], device_id=s_peer(d), device_id_type=MESH,
        )

    for d in (4, 3, 5, 2, 6, 1, 7):
        p2_copy(d).start()
    mine, theirs = p2s[s].astype(F32), None
    for d in (1, 7, 2, 6, 3, 5, 4):
        p2_copy(d).wait_recv()
        block = p2r[d].astype(F32)
        if d % 2 == 0:
            mine = mine + block
        else:
            theirs = block if theirs is None else theirs + block

    for i in range(Z):
        p3s[c, i] = mine[i : i + 1]
        p3s[1 - c, i] = theirs[i : i + 1]

    def p3_copy(d):
        return pltpu.make_async_remote_copy(
            src_ref=p3s.at[:, lax.rem(z + d, Z)], dst_ref=p3r.at[d], send_sem=p3_send.at[d],
            recv_sem=p3_recv.at[d], device_id=z_peer(d), device_id_type=MESH,
        )

    for d in (6, 5, 7, 4, 8, 3, 9, 2, 10, 1, 11):
        p3_copy(d).start()
    row = p3s[:, z]
    for d in (1, 11, 2, 10, 3, 9, 4, 8, 5, 7, 6):
        p3_copy(d).wait_recv()
        row = row + p3r[d]
    row = row * norm
    grad_out[:, : 2 * VAL] = row[0]
    grad_out[:, 2 * VAL :] = row[1]

    cols = pl.ds(0, COL)
    for n in range(D // COL):
        pltpu.make_async_copy(enc.at[n], enc_out.at[0, :, :, cols], enc_sem.at[n]).wait()
    for copy in direct + relays + [q_copy]:
        copy.wait_send()
    for i in range(1, 8):
        p1_copy(i // 2, i % 2).wait_send()
        p2_copy(i).wait_send()
    for d in range(1, Z):
        p3_copy(d).wait_send()


def per_device(dna, dw, pw, qw, kw, vw, cot):
    norm = 1.0 / math.sqrt(X * Z * dna.shape[1])
    dma = pltpu.SemaphoreType.DMA
    vmem = pltpu.VMEM
    anywhere = pl.BlockSpec(memory_space=pl.ANY)
    return pl.pallas_call(
        functools.partial(kernel, norm),
        out_shape=(
            jax.ShapeDtypeStruct((1, 2, ROWS, D), BF16),
            jax.ShapeDtypeStruct((1, 4 * VAL), F32),
        ),
        in_specs=[anywhere] * 7,
        out_specs=(anywhere, pl.BlockSpec(memory_space=pltpu.VMEM)),
        scratch_shapes=[
            vmem((2, 2 * ROWS, C_IN), BF16),
            vmem((3, C_IN), BF16),
            vmem((C_IN, D), BF16),
            vmem((D, 4 * KEY), BF16),
            vmem((D, KEY), BF16),
            vmem((D, VAL), BF16),
            vmem((2, ROWS, C_IN), BF16),
            vmem((6, 2 * ROWS, LANE), F32),
            vmem((12, ROWS + 16, LANE), F32),
            vmem((2 * ROWS, C_IN), BF16),
            vmem((D // COL, 2, ROWS, COL), BF16),
            vmem((2 * ROWS, LANE), F32),
            vmem((2, ROWS, LANE), F32),
            vmem((ROWS, 4 * KEY), F32),
            vmem((2 * ROWS, KEY), F32),
            vmem((2 * ROWS, VAL), F32),
            vmem((2, 12, 1, LANE), F32),
            vmem((2, 12, 1, LANE), F32),
            vmem((4, ROWS, KEY), BF16),
            vmem((2, 2, ROWS, KEY), BF16),
            vmem((2, ROWS, KV_W), BF16),
            vmem((8, ROWS, KV_W), BF16),
            vmem((4 * ROWS, COL), F32),
            vmem((X, 2 * ROWS, 2 * ROWS), BF16),
            vmem((2 * ROWS, 2 * VAL), BF16),
            vmem((8, Z * S, 2 * VAL), BF16),
            vmem((8, Z * S, 2 * VAL), BF16),
            vmem((3, 16 * S, LANE), F32),
            vmem((S, 16, 2 * VAL), BF16),
            vmem((S, 16, 2 * VAL), BF16),
            vmem((2, Z, 1, 2 * VAL), F32),
            vmem((Z, 2, 1, 2 * VAL), F32),
            dma((7,)), dma((D // COL,)), dma((2,)), dma((2,)), dma, dma, dma, dma,
            dma((3,)), dma((3,)), dma((4,)), dma((4,)), dma((8,)), dma((8,)), dma((8,)), dma((8,)),
            dma((Z,)), dma((Z,)),
        ],
        compiler_params=pltpu.CompilerParams(
            collective_id=0, has_side_effects=True, vmem_limit_bytes=40 * 2**20
        ),
        name="window_step",
    )(dna, dw, pw, qw, kw, vw, cot)


def solution(mesh):
    rows = P("batch", None, "seq", None)
    return jax.shard_map(
        per_device,
        mesh=mesh,
        in_specs=(rows, P(), P(), P(), P(), P(), rows),
        out_specs=(rows, P(("batch", "segment", "seq"), None)),
        check_vma=False,
    )
```

```python
import functools
import math

import jax
import jax.numpy as jnp
from jax import lax
from jax.experimental import pallas as pl
from jax.experimental.pallas import tpu as pltpu
from jax.sharding import PartitionSpec as P

MESH = pl.DeviceIdType.MESH
F32 = jnp.float32
BF16 = jnp.bfloat16

C_IN = 768
D = 1536
KEY = 128
VAL = 192
ROWS = 96
X, Z, S = 4, 12, 8
EPSILON = 1e-06
LANE = 128
COL = 256
KV_ROWS = 2 * ROWS + ROWS // 2
EXP2_SCALE = math.log2(math.e) / math.sqrt(KEY)


def gelu(u):
    inner = math.sqrt(2.0 / math.pi) * (u + 0.044715 * (u * u * u))
    return 0.5 * u * (1.0 + jnp.tanh(inner))


def rms_of(values):
    return lax.rsqrt(jnp.mean(values * values, axis=-1, keepdims=True) + EPSILON)


def kernel(
    norm,
    dna, dw, pw, qw, kw, vw, cot,
    enc_out, grad_out,
    xin, dwv, pwv, qwv, kwv, vwv, cotv,
    xf, ext, pooled, enc, ssq, rinv, qacc, kacc, vacc,
    hs, hr, q4, qall, kvs, kvbuf, acc, cott, attx, psend, p1r, red1, p2s, p2r, p3s, p3r,
    in_sem, enc_sem, h_send, h_recv, cot_send, cot_recv, q_send, q_recv,
    d_send, d_recv, r_send, r_recv, a_send, a_recv,
    p1_send, p1_recv, p2_send, p2_recv, p3_send, p3_recv, met1, met2, met3,
):
    b, g, s = lax.axis_index("batch"), lax.axis_index("segment"), lax.axis_index("seq")
    x, z = b // Z, lax.rem(b, Z)
    h, c = s // 2, lax.rem(s, 2)
    other = 1 - g
    sign = 2 * g - 1

    def x_peer(d):
        return (lax.rem(x + d, X) * Z + z, g, s)

    def s_peer(d):
        return (b, g, lax.rem(s + d, S))

    def z_peer(d):
        return (x * Z + lax.rem(z + d, Z), g, s)

    sib = (b, g, h * 2 + (1 - c))
    partner = (b, other, s)
    near = (b, other, lax.rem(h + sign + 4, 4) * 2 + c)
    ahead = (b, g, lax.rem(h + sign + 4, 4) * 2 + c)
    behind = (b, g, lax.rem(h - sign + 4, 4) * 2 + c)
    cross = (b, g, lax.rem(s + 2 * c - 1 + S, S))

    def signal(semaphore, devices):
        for device in devices:
            pl.semaphore_signal(semaphore, inc=1, device_id=device, device_id_type=MESH)

    barrier = pltpu.get_barrier_semaphore()
    beside = [partner, near, x_peer(1), x_peer(X - 1), z_peer(1), z_peer(Z - 1)]
    signal(barrier, [cross, sib] + beside)

    loads = [
        pltpu.make_async_copy(dna.at[0], xin, in_sem.at[0]),
        pltpu.make_async_copy(dw, dwv, in_sem.at[1]),
        pltpu.make_async_copy(pw, pwv, in_sem.at[2]),
        pltpu.make_async_copy(kw, kwv, in_sem.at[3]),
        pltpu.make_async_copy(vw, vwv, in_sem.at[4]),
        pltpu.make_async_copy(qw, qwv, in_sem.at[5]),
        pltpu.make_async_copy(cot.at[0, g], cotv.at[0, 0], in_sem.at[6]),
        pltpu.make_async_copy(cot.at[0, other], cotv.at[1, 0], in_sem.at[7]),
    ]
    for load in loads:
        load.start()

    loads[0].wait()
    for m in range(2):
        for k in range(6):
            i = m * 6 + k
            xf[k] = xin[m, :, k * LANE : (k + 1) * LANE].astype(F32)
            even = xf[k, pl.ds(0, ROWS, stride=2), :]
            ext[i, 8 : 8 + ROWS, :] = even
            hs[0, i] = even[0:1]
            hs[1, i] = even[ROWS - 1 : ROWS]

    pl.semaphore_wait(barrier, 8)
    to_left = pltpu.make_async_remote_copy(
        src_ref=hs.at[0], dst_ref=hr.at[1], send_sem=h_send.at[0], recv_sem=h_recv.at[1],
        device_id=s_peer(S - 1), device_id_type=MESH,
    )
    to_right = pltpu.make_async_remote_copy(
        src_ref=hs.at[1], dst_ref=hr.at[0], send_sem=h_send.at[1], recv_sem=h_recv.at[0],
        device_id=s_peer(1), device_id_type=MESH,
    )
    to_left.start()
    to_right.start()
    signal(met1, beside)
    loads[1].wait()
    w = dwv[...].astype(F32)
    to_left.wait()
    to_right.wait()

    for m in range(2):
        for k in range(6):
            i = m * 6 + k
            ext[i, 7:8, :] = jnp.where(s > 0, hr[0, i], 0.0)
            ext[i, 8 + ROWS : 9 + ROWS, :] = jnp.where(s < S - 1, hr[1, i], 0.0)
            part = slice(k * LANE, (k + 1) * LANE)
            total = w[0:1, part] * ext[i, 7 : 7 + ROWS, :]
            total = total + w[1:2, part] * ext[i, 8 : 8 + ROWS, :]
            total = total + w[2:3, part] * ext[i, 9 : 9 + ROWS, :]
            pooled[m * ROWS : (m + 1) * ROWS, part] = total.astype(BF16)

    pl.semaphore_wait(met1, 6)
    signal(met2, [ahead, behind, z_peer(2), z_peer(Z - 2)])
    loads[6].wait()
    loads[7].wait()
    cot_copy = pltpu.make_async_remote_copy(
        src_ref=cotv.at[:, 0], dst_ref=cotv.at[:, 1], send_sem=cot_send, recv_sem=cot_recv,
        device_id=sib, device_id_type=MESH,
    )
    cot_copy.start()
    for load in loads[2:6]:
        load.wait()

    for n in range(D // COL):
        cols = slice(n * COL, (n + 1) * COL)
        u = jnp.dot(pooled[...], pwv[:, cols], preferred_element_type=F32)
        rows = gelu(u).astype(BF16)
        enc[n] = rows.reshape(2, ROWS, COL)
        pltpu.make_async_copy(enc.at[n], enc_out.at[0, :, :, cols], enc_sem.at[n]).start()
        wide = rows.astype(F32)
        square = wide * wide
        square = square[:, :LANE] + square[:, LANE:]
        key_part = jnp.dot(rows, kwv[cols, :], preferred_element_type=F32)
        value_part = lax.dot_general(
            rows, vwv[:, cols], (((1,), (1,)), ((), ())), preferred_element_type=F32
        )
        query_part = jnp.dot(enc[n, g], qwv[cols, :], preferred_element_type=F32)
        if n == 0:
            ssq[...], kacc[...], vacc[...], qacc[...] = square, key_part, value_part, query_part
        else:
            ssq[...] += square
            kacc[...] += key_part
            vacc[...] += value_part
            qacc[...] += query_part

    scale = lax.rsqrt(jnp.sum(ssq[...], axis=-1, keepdims=True) * (1.0 / D) + EPSILON)
    rinv[...] = jnp.broadcast_to(scale, (2 * ROWS, LANE)).reshape(2, ROWS, LANE)
    keys = kacc[...] * scale
    keys = (keys * rms_of(keys)).astype(BF16)
    values = (vacc[...] * scale).astype(BF16)
    half = ROWS // 2
    for m in range(2):
        value = values[m * ROWS : (m + 1) * ROWS]
        kvs[m, :ROWS] = keys[m * ROWS : (m + 1) * ROWS]
        kvs[m, ROWS : 2 * ROWS] = value[:, :LANE]
        kvs[m, 2 * ROWS :] = jnp.concatenate([value[:half, LANE:], value[half:, LANE:]], axis=1)

    def kv_copy(j, source, slot, device):
        return pltpu.make_async_remote_copy(
            src_ref=source, dst_ref=kvbuf.at[slot], send_sem=d_send.at[j],
            recv_sem=d_recv.at[j], device_id=device, device_id_type=MESH,
        )

    def relay(j, source):
        return pltpu.make_async_remote_copy(
            src_ref=source, dst_ref=kvbuf.at[2 * j + 1], send_sem=r_send.at[j],
            recv_sem=r_recv.at[j], device_id=sib, device_id_type=MESH,
        )

    direct = [
        kv_copy(0, kvs.at[other], 2, near),
        kv_copy(1, kvs.at[g], 4, ahead),
        kv_copy(2, kvbuf.at[2], 6, behind),
    ]
    direct[0].start()
    direct[1].start()
    relays = [relay(0, kvs.at[g])] + [relay(j, kvbuf.at[2 * j]) for j in range(1, 4)]
    relays[0].start()
    kvbuf[0] = kvs[g]

    row_scale = rinv[g]
    for i in range(4):
        query = qacc[:, i * KEY : (i + 1) * KEY] * row_scale
        q4[i] = (query * rms_of(query)).astype(BF16)
    q_copy = pltpu.make_async_remote_copy(
        src_ref=q4.at[pl.ds(2 * (1 - c), 2)], dst_ref=qall.at[:, 1], send_sem=q_send,
        recv_sem=q_recv, device_id=sib, device_id_type=MESH,
    )
    q_copy.start()
    qall[:, 0] = q4[pl.ds(2 * c, 2)]

    pl.semaphore_wait(met2, 4)
    signal(met3, [sib, z_peer(2), z_peer(Z - 2)])

    direct[0].wait_recv()
    direct[2].start()
    relays[1].start()

    cot_copy.wait()
    for k in range(6):
        wide = cotv[:, :, :, k * LANE : (k + 1) * LANE].astype(F32).reshape(4 * ROWS, LANE)
        turned = jnp.transpose(wide).reshape(8, 2, S, 4 * ROWS)
        turned = jnp.where(g == 0, turned[:, 0], turned[:, 1])
        cott[k * 64 : (k + 1) * 64] = turned.reshape(64, 4 * ROWS).astype(BF16)

    ones = jnp.ones((half, 2 * LANE - VAL), BF16)

    def group(j):
        key = kvbuf[2 * j : 2 * j + 2, :ROWS].reshape(2 * ROWS, KEY)
        head = kvbuf[2 * j : 2 * j + 2, ROWS : 2 * ROWS].reshape(2 * ROWS, LANE)
        tails = []
        for i in range(2):
            tail = kvbuf[2 * j + i, 2 * ROWS :]
            tails.append(jnp.concatenate([tail[:, : VAL - LANE], ones], axis=1))
            tails.append(jnp.concatenate([tail[:, VAL - LANE :], ones], axis=1))
        return key, jnp.concatenate([head, jnp.concatenate(tails, axis=0)], axis=1)

    def attend(query, key, value):
        scores = lax.dot_general(
            query, key, (((1,), (1,)), ((), ())), preferred_element_type=F32
        )
        weights = jnp.exp2(scores * EXP2_SCALE).astype(BF16)
        return jnp.dot(weights, value, preferred_element_type=F32)

    q_copy.wait_recv()
    relays[0].wait_recv()
    query = qall[...].reshape(4 * ROWS, KEY)
    acc[...] = attend(query, *group(0))
    direct[1].wait_recv()
    relays[2].start()
    relays[1].wait_recv()
    acc[...] += attend(query, *group(1))
    direct[2].wait_recv()
    relays[3].start()
    relays[2].wait_recv()
    acc[...] += attend(query, *group(2))
    relays[3].wait_recv()
    last = group(3)

    def att_copy(i):
        return pltpu.make_async_remote_copy(
            src_ref=attx.at[i], dst_ref=attx.at[2 + i], send_sem=a_send.at[i],
            recv_sem=a_recv.at[i], device_id=partner, device_id_type=MESH,
        )

    for i in range(2):
        heads = []
        for j in range(2):
            at = (j * 2 + i) * ROWS
            total = acc[at : at + ROWS] + attend(qall[j, i], *last)
            heads.append(total[:, :VAL] / total[:, VAL : VAL + 1])
        attx[i] = jnp.concatenate(heads, axis=1).astype(BF16)
        att_copy(i).start()
    for i in range(2):
        att_copy(i).wait_recv()

    def p1_copy(d):
        return pltpu.make_async_remote_copy(
            src_ref=psend.at[d], dst_ref=p1r.at[d], send_sem=p1_send.at[d],
            recv_sem=p1_recv.at[d], device_id=x_peer(d), device_id_type=MESH,
        )

    def share(d):
        rows = pl.ds(pl.multiple_of(lax.rem(x + d, X) * ROWS, ROWS), ROWS)
        return jnp.dot(
            cott[rows, :], attx[...].reshape(4 * ROWS, 2 * VAL), preferred_element_type=F32
        )

    for d in (2, 1, 3):
        psend[d] = share(d).astype(BF16)
        p1_copy(d).start()
    total = share(0)
    pl.semaphore_wait(met3, 3)
    for d in (1, 3, 2):
        p1_copy(d).wait_recv()
        total = total + p1r[d].astype(F32)

    for k in range(3):
        red1[k, : Z * S, :] = total[:, k * LANE : (k + 1) * LANE]
        red1[k, Z * S :, :] = jnp.zeros((S * 16 - Z * S, LANE), F32)
    for i in range(S):
        for k in range(3):
            p2s[i, :, k * LANE : (k + 1) * LANE] = red1[k, pl.ds(i, 16, stride=S), :].astype(BF16)

    def p2_copy(d):
        return pltpu.make_async_remote_copy(
            src_ref=p2s.at[lax.rem(s + d, S)], dst_ref=p2r.at[d], send_sem=p2_send.at[d],
            recv_sem=p2_recv.at[d], device_id=s_peer(d), device_id_type=MESH,
        )

    for d in (4, 3, 5, 2, 6, 1, 7):
        p2_copy(d).start()
    mine, theirs = p2s[s].astype(F32), None
    for d in (1, 7, 2, 6, 3, 5, 4):
        p2_copy(d).wait_recv()
        block = p2r[d].astype(F32)
        if d % 2 == 0:
            mine = mine + block
        else:
            theirs = block if theirs is None else theirs + block

    for i in range(Z):
        p3s[c, i] = mine[i : i + 1]
        p3s[1 - c, i] = theirs[i : i + 1]

    def p3_copy(d):
        return pltpu.make_async_remote_copy(
            src_ref=p3s.at[:, lax.rem(z + d, Z)], dst_ref=p3r.at[d], send_sem=p3_send.at[d],
            recv_sem=p3_recv.at[d], device_id=z_peer(d), device_id_type=MESH,
        )

    for d in (6, 5, 7, 4, 8, 3, 9, 2, 10, 1, 11):
        p3_copy(d).start()
    row = p3s[:, z]
    for d in (1, 11, 2, 10, 3, 9, 4, 8, 5, 7, 6):
        p3_copy(d).wait_recv()
        row = row + p3r[d]
    row = row * norm
    grad_out[:, : 2 * VAL] = row[0]
    grad_out[:, 2 * VAL :] = row[1]

    cols = pl.ds(0, COL)
    for n in range(D // COL):
        pltpu.make_async_copy(enc.at[n], enc_out.at[0, :, :, cols], enc_sem.at[n]).wait()
    for copy in direct + relays + [q_copy, att_copy(0), att_copy(1)]:
        copy.wait_send()
    for d in range(1, X):
        p1_copy(d).wait_send()
    for d in range(1, S):
        p2_copy(d).wait_send()
    for d in range(1, Z):
        p3_copy(d).wait_send()


def per_device(dna, dw, pw, qw, kw, vw, cot):
    norm = 1.0 / math.sqrt(X * Z * dna.shape[1])
    dma = pltpu.SemaphoreType.DMA
    vmem = pltpu.VMEM
    hbm = pl.BlockSpec(memory_space=pltpu.MemorySpace.HBM)
    return pl.pallas_call(
        functools.partial(kernel, norm),
        out_shape=(
            jax.ShapeDtypeStruct((1, 2, ROWS, D), BF16),
            jax.ShapeDtypeStruct((1, 4 * VAL), F32),
        ),
        in_specs=[hbm] * 7,
        out_specs=(hbm, pl.BlockSpec(memory_space=pltpu.VMEM)),
        scratch_shapes=[
            vmem((2, 2 * ROWS, C_IN), BF16),
            vmem((3, C_IN), BF16),
            vmem((C_IN, D), BF16),
            vmem((D, 4 * KEY), BF16),
            vmem((D, KEY), BF16),
            vmem((VAL, D), BF16),
            vmem((2, 2, ROWS, C_IN), BF16),
            vmem((6, 2 * ROWS, LANE), F32),
            vmem((12, ROWS + 16, LANE), F32),
            vmem((2 * ROWS, C_IN), BF16),
            vmem((D // COL, 2, ROWS, COL), BF16),
            vmem((2 * ROWS, LANE), F32),
            vmem((2, ROWS, LANE), F32),
            vmem((ROWS, 4 * KEY), F32),
            vmem((2 * ROWS, KEY), F32),
            vmem((2 * ROWS, VAL), F32),
            vmem((2, 12, 1, LANE), F32),
            vmem((2, 12, 1, LANE), F32),
            vmem((4, ROWS, KEY), BF16),
            vmem((2, 2, ROWS, KEY), BF16),
            vmem((2, KV_ROWS, LANE), BF16),
            vmem((8, KV_ROWS, LANE), BF16),
            vmem((4 * ROWS, 2 * LANE), F32),
            vmem((X * ROWS, 4 * ROWS), BF16),
            vmem((4, ROWS, 2 * VAL), BF16),
            vmem((X, ROWS, 2 * VAL), BF16),
            vmem((X, ROWS, 2 * VAL), BF16),
            vmem((3, 16 * S, LANE), F32),
            vmem((S, 16, 2 * VAL), BF16),
            vmem((S, 16, 2 * VAL), BF16),
            vmem((2, Z, 1, 2 * VAL), F32),
            vmem((Z, 2, 1, 2 * VAL), F32),
            dma((8,)), dma((D // COL,)), dma((2,)), dma((2,)), dma, dma, dma, dma,
            dma((3,)), dma((3,)), dma((4,)), dma((4,)), dma((2,)), dma((2,)),
            dma((X,)), dma((X,)), dma((S,)), dma((S,)), dma((Z,)), dma((Z,)),
            pltpu.SemaphoreType.REGULAR, pltpu.SemaphoreType.REGULAR, pltpu.SemaphoreType.REGULAR,
        ],
        compiler_params=pltpu.CompilerParams(
            collective_id=0, has_side_effects=True, vmem_limit_bytes=62 * 2**20
        ),
        name="window_step",
    )(dna, dw, pw, qw, kw, vw.T, cot)


def solution(mesh):
    rows = P("batch", None, "seq", None)
    return jax.shard_map(
        per_device,
        mesh=mesh,
        in_specs=(rows, P(), P(), P(), P(), P(), rows),
        out_specs=(rows, P(("batch", "segment", "seq"), None)),
        check_vma=False,
    )
```

```python
import functools
import math

import jax
import jax.numpy as jnp
from jax import lax
from jax.experimental import pallas as pl
from jax.experimental.pallas import tpu as pltpu
from jax.sharding import PartitionSpec as P

MESH = pl.DeviceIdType.MESH
F32 = jnp.float32
BF16 = jnp.bfloat16

C_IN = 768
D = 1536
KEY = 128
VAL = 192
ROWS = 96
X, Z, S = 4, 12, 8
EPSILON = 1e-06
LANE = 128
COL = 256
KV_ROWS = 2 * ROWS + ROWS // 2
EXP2_SCALE = math.log2(math.e) / math.sqrt(KEY)


def gelu(u):
    inner = math.sqrt(2.0 / math.pi) * (u + 0.044715 * (u * u * u))
    return 0.5 * u * (1.0 + jnp.tanh(inner))


def rms_of(values):
    return lax.rsqrt(jnp.mean(values * values, axis=-1, keepdims=True) + EPSILON)


def kernel(
    norm,
    dna, dw, pw, qw, kw, vw, cot,
    enc_out, grad_out,
    xin, dwv, pwv, qwv, kwv, vwv, cotv,
    xf, ext, pooled, edge, enc,
    hs, hr, q4, qall, kvs, kvbuf, acc, cott, attx, own, psend, p1r, red1, p2s, p2r, p3s, p3r,
    in_sem, enc_sem, h_send, h_recv, cot_send, cot_recv, q_send, q_recv,
    d_send, d_recv, r_send, r_recv, a_send, a_recv,
    p1_send, p1_recv, p2_send, p2_recv, p3_send, p3_recv, met1, met2, met3,
):
    b, g, s = lax.axis_index("batch"), lax.axis_index("segment"), lax.axis_index("seq")
    x, z = b // Z, lax.rem(b, Z)
    h, c = s // 2, lax.rem(s, 2)
    other = 1 - g
    sign = 2 * g - 1

    def x_peer(d):
        return (lax.rem(x + d, X) * Z + z, g, s)

    def s_peer(d):
        return (b, g, lax.rem(s + d, S))

    def z_peer(d):
        return (x * Z + lax.rem(z + d, Z), g, s)

    sib = (b, g, h * 2 + (1 - c))
    partner = (b, other, s)
    near = (b, other, lax.rem(h + sign + 4, 4) * 2 + c)
    ahead = (b, g, lax.rem(h + sign + 4, 4) * 2 + c)
    behind = (b, g, lax.rem(h - sign + 4, 4) * 2 + c)
    cross = (b, g, lax.rem(s + 2 * c - 1 + S, S))

    def signal(semaphore, devices):
        for device in devices:
            pl.semaphore_signal(semaphore, inc=1, device_id=device, device_id_type=MESH)

    barrier = pltpu.get_barrier_semaphore()
    beside = [partner, near, x_peer(1), x_peer(X - 1), z_peer(1), z_peer(Z - 1)]
    signal(barrier, [cross, sib] + beside)

    loads = [
        pltpu.make_async_copy(dna.at[0], xin, in_sem.at[0]),
        pltpu.make_async_copy(dw, dwv, in_sem.at[1]),
        pltpu.make_async_copy(pw, pwv, in_sem.at[2]),
        pltpu.make_async_copy(kw, kwv, in_sem.at[3]),
        pltpu.make_async_copy(vw, vwv, in_sem.at[4]),
        pltpu.make_async_copy(qw, qwv, in_sem.at[5]),
        pltpu.make_async_copy(cot.at[0, g], cotv.at[0, 0], in_sem.at[6]),
        pltpu.make_async_copy(cot.at[0, other], cotv.at[1, 0], in_sem.at[7]),
    ]
    for load in loads:
        load.start()

    loads[0].wait()
    for m in range(2):
        for k in range(6):
            i = m * 6 + k
            xf[k] = xin[m, :, k * LANE : (k + 1) * LANE].astype(F32)
            even = xf[k, pl.ds(0, ROWS, stride=2), :]
            ext[i, 7:8, :] = jnp.zeros((1, LANE), F32)
            ext[i, 8 : 8 + ROWS, :] = even
            ext[i, 8 + ROWS : 9 + ROWS, :] = jnp.zeros((1, LANE), F32)
            hs[0, i] = even[0:1]
            hs[1, i] = even[ROWS - 1 : ROWS]

    pl.semaphore_wait(barrier, 8)
    to_left = pltpu.make_async_remote_copy(
        src_ref=hs.at[0], dst_ref=hr.at[1], send_sem=h_send.at[0], recv_sem=h_recv.at[1],
        device_id=s_peer(S - 1), device_id_type=MESH,
    )
    to_right = pltpu.make_async_remote_copy(
        src_ref=hs.at[1], dst_ref=hr.at[0], send_sem=h_send.at[1], recv_sem=h_recv.at[0],
        device_id=s_peer(1), device_id_type=MESH,
    )
    to_left.start()
    to_right.start()
    signal(met1, beside)
    loads[1].wait()
    w = dwv[...].astype(F32)
    for m in range(2):
        for k in range(6):
            i = m * 6 + k
            part = slice(k * LANE, (k + 1) * LANE)
            total = w[0:1, part] * ext[i, 7 : 7 + ROWS, :]
            total = total + w[1:2, part] * ext[i, 8 : 8 + ROWS, :]
            total = total + w[2:3, part] * ext[i, 9 : 9 + ROWS, :]
            pooled[m * ROWS : (m + 1) * ROWS, part] = total.astype(BF16)
    loads[2].wait()
    for n in range(D // COL):
        cols = slice(n * COL, (n + 1) * COL)
        u = jnp.dot(pooled[...], pwv[:, cols], preferred_element_type=F32)
        enc[n] = gelu(u).astype(BF16).reshape(2, ROWS, COL)

    pl.semaphore_wait(met1, 6)
    signal(met2, [ahead, behind, z_peer(2), z_peer(Z - 2)])
    loads[6].wait()
    loads[7].wait()
    cot_copy = pltpu.make_async_remote_copy(
        src_ref=cotv.at[:, 0], dst_ref=cotv.at[:, 1], send_sem=cot_send, recv_sem=cot_recv,
        device_id=sib, device_id_type=MESH,
    )
    cot_copy.start()

    to_left.wait()
    to_right.wait()
    edge[...] = jnp.zeros_like(edge)
    for m in range(2):
        for k in range(6):
            i = m * 6 + k
            part = slice(k * LANE, (k + 1) * LANE)
            before = jnp.where(s > 0, hr[0, i], 0.0)
            after = jnp.where(s < S - 1, hr[1, i], 0.0)
            total = w[0:1, part] * before + w[1:2, part] * ext[i, 8:9, :]
            edge[2 * m : 2 * m + 1, part] = total + w[2:3, part] * ext[i, 9:10, :]
            end = 7 + ROWS
            total = w[0:1, part] * ext[i, end - 1 : end, :] + w[1:2, part] * ext[i, end : end + 1, :]
            edge[2 * m + 1 : 2 * m + 2, part] = total + w[2:3, part] * after
    edge_rows = edge[...].astype(BF16)
    row = lax.broadcasted_iota(jnp.int32, (16, COL), 0)
    for n in range(D // COL):
        cols = slice(n * COL, (n + 1) * COL)
        u = gelu(jnp.dot(edge_rows, pwv[:, cols], preferred_element_type=F32))
        for m in range(2):
            first = jnp.where(row == 0, u[2 * m : 2 * m + 1], enc[n, m, :16].astype(F32))
            enc[n, m, :16] = first.astype(BF16)
            final = jnp.where(row == 15, u[2 * m + 1 : 2 * m + 2], enc[n, m, ROWS - 16 :].astype(F32))
            enc[n, m, ROWS - 16 :] = final.astype(BF16)
        pltpu.make_async_copy(enc.at[n], enc_out.at[0, :, :, cols], enc_sem.at[n]).start()

    for load in loads[3:6]:
        load.wait()
    half = ROWS // 2

    def rows_of(micro):
        rows = jnp.concatenate([enc[n, micro] for n in range(D // COL)], axis=1)
        total = jnp.zeros((ROWS, LANE), F32)
        for n in range(D // LANE):
            wide = rows[:, n * LANE : (n + 1) * LANE].astype(F32)
            total = total + wide * wide
        return rows, lax.rsqrt(jnp.sum(total, axis=-1, keepdims=True) * (1.0 / D) + EPSILON)

    def project(micro):
        rows, scale = rows_of(micro)
        key = jnp.dot(rows, kwv[...], preferred_element_type=F32) * scale
        value = lax.dot_general(
            rows, vwv[...], (((1,), (1,)), ((), ())), preferred_element_type=F32
        )
        value = (value * scale).astype(BF16)
        kvs[micro, :ROWS] = (key * rms_of(key)).astype(BF16)
        kvs[micro, ROWS : 2 * ROWS] = value[:, :LANE]
        kvs[micro, 2 * ROWS :] = jnp.concatenate([value[:half, LANE:], value[half:, LANE:]], axis=1)
        return rows, scale

    def kv_copy(j, source, slot, device, part=slice(None)):
        return pltpu.make_async_remote_copy(
            src_ref=source.at[part], dst_ref=kvbuf.at[slot, part], send_sem=d_send.at[j],
            recv_sem=d_recv.at[j], device_id=device, device_id_type=MESH,
        )

    def relay(j, source):
        return pltpu.make_async_remote_copy(
            src_ref=source, dst_ref=kvbuf.at[2 * j + 1], send_sem=r_send.at[j],
            recv_sem=r_recv.at[j], device_id=sib, device_id_type=MESH,
        )

    parts = (pl.ds(0, 112), pl.ds(112, KV_ROWS - 112))
    to_near = [kv_copy(j, kvs.at[other], 2, near, part) for j, part in enumerate(parts)]
    forward = [kv_copy(2 + j, kvbuf.at[2], 6, behind, part) for j, part in enumerate(parts)]
    to_ahead = kv_copy(4, kvs.at[g], 4, ahead)
    project(other)
    to_near[0].start()
    to_near[1].start()
    rows, scale = project(g)
    to_ahead.start()
    relays = [relay(0, kvs.at[g])] + [relay(j, kvbuf.at[2 * j]) for j in range(1, 4)]
    relays[0].start()
    kvbuf[0] = kvs[g]

    queries = jnp.dot(rows, qwv[...], preferred_element_type=F32) * scale
    for i in range(4):
        query = queries[:, i * KEY : (i + 1) * KEY]
        q4[i] = (query * rms_of(query)).astype(BF16)
    q_copy = pltpu.make_async_remote_copy(
        src_ref=q4.at[pl.ds(2 * (1 - c), 2)], dst_ref=qall.at[:, 1], send_sem=q_send,
        recv_sem=q_recv, device_id=sib, device_id_type=MESH,
    )
    q_copy.start()
    qall[:, 0] = q4[pl.ds(2 * c, 2)]

    pl.semaphore_wait(met2, 4)
    signal(met3, [sib, z_peer(2), z_peer(Z - 2)])

    def turn(k):
        wide = cotv[:, :, :, k * LANE : (k + 1) * LANE].astype(F32).reshape(4 * ROWS, LANE)
        turned = jnp.transpose(wide).reshape(8, 2, S, 4 * ROWS)
        turned = jnp.where(g == 0, turned[:, 0], turned[:, 1])
        cott[k * 64 : (k + 1) * 64] = turned.reshape(64, 4 * ROWS).astype(BF16)

    cot_copy.wait()
    for j in range(2):
        to_near[j].wait_recv()
        forward[j].start()
        if j == 1:
            relays[1].start()
        for k in range(3):
            turn(3 * j + k)

    ones = jnp.ones((half, 2 * LANE - VAL), BF16)

    def group(j):
        key = kvbuf[2 * j : 2 * j + 2, :ROWS].reshape(2 * ROWS, KEY)
        head = kvbuf[2 * j : 2 * j + 2, ROWS : 2 * ROWS].reshape(2 * ROWS, LANE)
        tails = []
        for i in range(2):
            tail = kvbuf[2 * j + i, 2 * ROWS :]
            tails.append(jnp.concatenate([tail[:, : VAL - LANE], ones], axis=1))
            tails.append(jnp.concatenate([tail[:, VAL - LANE :], ones], axis=1))
        return key, jnp.concatenate([head, jnp.concatenate(tails, axis=0)], axis=1)

    def attend(query, key, value):
        scores = lax.dot_general(
            query, key, (((1,), (1,)), ((), ())), preferred_element_type=F32
        )
        weights = jnp.exp2(scores * EXP2_SCALE).astype(BF16)
        return jnp.dot(weights, value, preferred_element_type=F32)

    q_copy.wait_recv()
    relays[0].wait_recv()
    query = qall[...].reshape(4 * ROWS, KEY)
    acc[...] = attend(query, *group(0))
    to_ahead.wait_recv()
    relays[2].start()
    relays[1].wait_recv()
    acc[...] += attend(query, *group(1))
    forward[0].wait_recv()
    forward[1].wait_recv()
    relays[3].start()
    relays[2].wait_recv()
    acc[...] += attend(query, *group(2))
    relays[3].wait_recv()
    last = group(3)

    def att_copy(t):
        return pltpu.make_async_remote_copy(
            src_ref=attx.at[t, :2], dst_ref=attx.at[t, 2:], send_sem=a_send.at[t],
            recv_sem=a_recv.at[t], device_id=partner, device_id_type=MESH,
        )

    def head(j, i):
        at = (j * 2 + i) * ROWS
        total = acc[at : at + ROWS] + attend(qall[j, i], *last)
        return (total[:, :VAL] / total[:, VAL : VAL + 1]).astype(BF16)

    low = [head(0, i) for i in range(2)]
    for i in range(2):
        attx[0, i] = low[i][:, :LANE]
    att_copy(0).start()
    high = [head(1, i) for i in range(2)]
    for i in range(2):
        attx[1, i] = jnp.concatenate([low[i][:, LANE:], high[i][:, : 2 * LANE - VAL]], axis=1)
    att_copy(1).start()
    for i in range(2):
        attx[2, i] = high[i][:, 2 * LANE - VAL :]
    att_copy(2).start()

    def share(t, first):
        part = cott[:, : 2 * ROWS] if first else cott[:, 2 * ROWS :]
        pair = attx[t, :2] if first else attx[t, 2:]
        part = jnp.dot(part, pair.reshape(2 * ROWS, LANE), preferred_element_type=F32)
        return part.reshape(X, ROWS, LANE)

    def p1_copy(t, d):
        return pltpu.make_async_remote_copy(
            src_ref=psend.at[t, lax.rem(x + d, X)], dst_ref=p1r.at[t, d],
            send_sem=p1_send.at[t, d], recv_sem=p1_recv.at[t, d],
            device_id=x_peer(d), device_id_type=MESH,
        )

    for t in range(3):
        own[t] = share(t, True)
    for t in range(3):
        att_copy(t).wait_recv()
        full = own[t] + share(t, False)
        own[t] = full
        psend[t] = full.astype(BF16)
        for d in (2, 1, 3):
            p1_copy(t, d).start()

    def p2_copy(t, d):
        return pltpu.make_async_remote_copy(
            src_ref=p2s.at[t, lax.rem(s + d, S)], dst_ref=p2r.at[t, d],
            send_sem=p2_send.at[t, d], recv_sem=p2_recv.at[t, d],
            device_id=s_peer(d), device_id_type=MESH,
        )

    pl.semaphore_wait(met3, 3)
    for t in range(3):
        total = own[t, x]
        for d in (1, 3, 2):
            p1_copy(t, d).wait_recv()
            total = total + p1r[t, d].astype(F32)
        red1[t, : Z * S, :] = total
        red1[t, Z * S :, :] = jnp.zeros((S * 16 - Z * S, LANE), F32)
        for i in range(S):
            p2s[t, i] = red1[t, pl.ds(i, 16, stride=S), :].astype(BF16)
        for d in (4, 3, 5, 2, 6, 1, 7):
            p2_copy(t, d).start()

    for t in range(3):
        mine, theirs = p2s[t, s].astype(F32), None
        for d in (1, 7, 2, 6, 3, 5, 4):
            p2_copy(t, d).wait_recv()
            block = p2r[t, d].astype(F32)
            if d % 2 == 0:
                mine = mine + block
            else:
                theirs = block if theirs is None else theirs + block
        part = slice(t * LANE, (t + 1) * LANE)
        for i in range(Z):
            p3s[c, i, :, part] = mine[i : i + 1]
            p3s[1 - c, i, :, part] = theirs[i : i + 1]

    def p3_copy(d):
        return pltpu.make_async_remote_copy(
            src_ref=p3s.at[:, lax.rem(z + d, Z)], dst_ref=p3r.at[d], send_sem=p3_send.at[d],
            recv_sem=p3_recv.at[d], device_id=z_peer(d), device_id_type=MESH,
        )

    for d in (6, 5, 7, 4, 8, 3, 9, 2, 10, 1, 11):
        p3_copy(d).start()
    row = p3s[:, z]
    for d in (1, 11, 2, 10, 3, 9, 4, 8, 5, 7, 6):
        p3_copy(d).wait_recv()
        row = row + p3r[d]
    row = row * norm
    grad_out[:, : 2 * VAL] = row[0]
    grad_out[:, 2 * VAL :] = row[1]

    cols = pl.ds(0, COL)
    for n in range(D // COL):
        pltpu.make_async_copy(enc.at[n], enc_out.at[0, :, :, cols], enc_sem.at[n]).wait()
    for copy in to_near + forward + [to_ahead] + relays + [q_copy]:
        copy.wait_send()
    for t in range(3):
        att_copy(t).wait_send()
        for d in range(1, X):
            p1_copy(t, d).wait_send()
        for d in range(1, S):
            p2_copy(t, d).wait_send()
    for d in range(1, Z):
        p3_copy(d).wait_send()


def deliver(encoded, grad, encoded_out, grad_out, rows, line, load_sem, store_sem):
    half = ROWS // 2
    places = []
    for i in range(4):
        at = (i // 2, pl.ds(i % 2 * half, half))
        places.append((encoded.at[0, *at], rows.at[at], encoded_out.at[0, *at]))
    places.append((grad, line, grad_out))
    loads = [
        pltpu.make_async_copy(source, held, load_sem.at[i])
        for i, (source, held, _) in enumerate(places)
    ]
    stores = [
        pltpu.make_async_copy(held, target, store_sem.at[i])
        for i, (_, held, target) in enumerate(places)
    ]
    for load in loads:
        load.start()
    for load, store in zip(loads, stores):
        load.wait()
        store.start()
    for store in stores:
        store.wait()


def per_device(dna, dw, pw, qw, kw, vw, cot):
    norm = 1.0 / math.sqrt(X * Z * dna.shape[1])
    dma = pltpu.SemaphoreType.DMA
    vmem = pltpu.VMEM
    hbm = pl.BlockSpec(memory_space=pltpu.MemorySpace.HBM)
    encoded, grad = pl.pallas_call(
        functools.partial(kernel, norm),
        out_shape=(
            jax.ShapeDtypeStruct((1, 2, ROWS, D), BF16),
            jax.ShapeDtypeStruct((1, 4 * VAL), F32),
        ),
        in_specs=[hbm] * 7,
        out_specs=(hbm, pl.BlockSpec(memory_space=pltpu.VMEM)),
        scratch_shapes=[
            vmem((2, 2 * ROWS, C_IN), BF16),
            vmem((3, C_IN), BF16),
            vmem((C_IN, D), BF16),
            vmem((D, 4 * KEY), BF16),
            vmem((D, KEY), BF16),
            vmem((VAL, D), BF16),
            vmem((2, 2, ROWS, C_IN), BF16),
            vmem((6, 2 * ROWS, LANE), F32),
            vmem((12, ROWS + 16, LANE), F32),
            vmem((2 * ROWS, C_IN), BF16),
            vmem((16, C_IN), F32),
            vmem((D // COL, 2, ROWS, COL), BF16),
            vmem((2, 12, 1, LANE), F32),
            vmem((2, 12, 1, LANE), F32),
            vmem((4, ROWS, KEY), BF16),
            vmem((2, 2, ROWS, KEY), BF16),
            vmem((2, KV_ROWS, LANE), BF16),
            vmem((8, KV_ROWS, LANE), BF16),
            vmem((4 * ROWS, 2 * LANE), F32),
            vmem((X * ROWS, 4 * ROWS), BF16),
            vmem((3, 4, ROWS, LANE), BF16),
            vmem((3, X, ROWS, LANE), F32),
            vmem((3, X, ROWS, LANE), BF16),
            vmem((3, X, ROWS, LANE), BF16),
            vmem((3, 16 * S, LANE), F32),
            vmem((3, S, 16, LANE), BF16),
            vmem((3, S, 16, LANE), BF16),
            vmem((2, Z, 1, 2 * VAL), F32),
            vmem((Z, 2, 1, 2 * VAL), F32),
            dma((8,)), dma((D // COL,)), dma((2,)), dma((2,)), dma, dma, dma, dma,
            dma((5,)), dma((5,)), dma((4,)), dma((4,)), dma((3,)), dma((3,)),
            dma((3, X)), dma((3, X)), dma((3, S)), dma((3, S)), dma((Z,)), dma((Z,)),
            pltpu.SemaphoreType.REGULAR, pltpu.SemaphoreType.REGULAR, pltpu.SemaphoreType.REGULAR,
        ],
        compiler_params=pltpu.CompilerParams(
            collective_id=0, has_side_effects=True, vmem_limit_bytes=62 * 2**20
        ),
        name="window_step",
    )(dna, dw, pw, qw, kw, vw.T, cot)
    return pl.pallas_call(
        deliver,
        out_shape=(
            jax.ShapeDtypeStruct(encoded.shape, BF16),
            jax.ShapeDtypeStruct(grad.shape, F32),
        ),
        in_specs=[hbm] * 2,
        out_specs=(hbm, hbm),
        scratch_shapes=[
            vmem((2, ROWS, D), BF16), vmem((1, 4 * VAL), F32), dma((5,)), dma((5,)),
        ],
        compiler_params=pltpu.CompilerParams(vmem_limit_bytes=62 * 2**20),
        name="deliver",
    )(encoded, grad)


def solution(mesh):
    rows = P("batch", None, "seq", None)
    return jax.shard_map(
        per_device,
        mesh=mesh,
        in_specs=(rows, P(), P(), P(), P(), P(), rows),
        out_specs=(rows, P(("batch", "segment", "seq"), None)),
        check_vma=False,
    )
```

```python
import functools
import math

import jax
import jax.numpy as jnp
from jax import lax
from jax.experimental import pallas as pl
from jax.experimental.pallas import tpu as pltpu
from jax.sharding import PartitionSpec as P

MESH = pl.DeviceIdType.MESH
F32 = jnp.float32
BF16 = jnp.bfloat16

C_IN = 768
D = 1536
KEY = 128
VAL = 192
ROWS = 96
X, Z, S = 4, 12, 8
EPSILON = 1e-06
LANE = 128
COL = 256
KV_ROWS = 2 * ROWS + ROWS // 2
EXP2_SCALE = math.log2(math.e) / math.sqrt(KEY)


def gelu(u):
    inner = math.sqrt(2.0 / math.pi) * (u + 0.044715 * (u * u * u))
    return 0.5 * u * (1.0 + jnp.tanh(inner))


def rms_of(values):
    return lax.rsqrt(jnp.mean(values * values, axis=-1, keepdims=True) + EPSILON)


def kernel(
    norm,
    dna, dw, pw, qw, kw, vw, cot,
    enc_out, grad_out,
    ein, xin, dwv, pwv, qwv, kwv, vwv, cotv,
    xf, ext, pooled, edge, enc,
    hs, hr, q4, qall, kvs, kvbuf, acc, cott, attx, own, psend, p1r, red1, p2s, p2r, p3s, p3r,
    in_sem, enc_sem, h_send, h_recv, cot_send, cot_recv, q_send, q_recv,
    d_send, d_recv, r_send, r_recv, a_send, a_recv,
    p1_send, p1_recv, p2_send, p2_recv, p3_send, p3_recv, met1, met2, met3,
):
    b, g, s = lax.axis_index("batch"), lax.axis_index("segment"), lax.axis_index("seq")
    x, z = b // Z, lax.rem(b, Z)
    h, c = s // 2, lax.rem(s, 2)
    other = 1 - g
    sign = 2 * g - 1

    def x_peer(d):
        return (lax.rem(x + d, X) * Z + z, g, s)

    def s_peer(d):
        return (b, g, lax.rem(s + d, S))

    def z_peer(d):
        return (x * Z + lax.rem(z + d, Z), g, s)

    sib = (b, g, h * 2 + (1 - c))
    partner = (b, other, s)
    near = (b, other, lax.rem(h + sign + 4, 4) * 2 + c)
    ahead = (b, g, lax.rem(h + sign + 4, 4) * 2 + c)
    behind = (b, g, lax.rem(h - sign + 4, 4) * 2 + c)
    cross = (b, g, lax.rem(s + 2 * c - 1 + S, S))

    def signal(semaphore, devices):
        for device in devices:
            pl.semaphore_signal(semaphore, inc=1, device_id=device, device_id_type=MESH)

    barrier = pltpu.get_barrier_semaphore()
    beside = [partner, near, x_peer(1), x_peer(X - 1), z_peer(1), z_peer(Z - 1)]
    signal(barrier, [cross, sib] + beside)

    ends = [
        pltpu.make_async_copy(dna.at[0, :, pl.ds(0, 16)], ein.at[0], in_sem.at[8]),
        pltpu.make_async_copy(dna.at[0, :, pl.ds(2 * ROWS - 16, 16)], ein.at[1], in_sem.at[9]),
    ]
    loads = [
        pltpu.make_async_copy(dna.at[0], xin, in_sem.at[0]),
        pltpu.make_async_copy(dw, dwv, in_sem.at[1]),
        pltpu.make_async_copy(pw, pwv, in_sem.at[2]),
        pltpu.make_async_copy(kw, kwv, in_sem.at[3]),
        pltpu.make_async_copy(vw, vwv, in_sem.at[4]),
        pltpu.make_async_copy(qw, qwv, in_sem.at[5]),
        pltpu.make_async_copy(cot.at[0, g], cotv.at[0, 0], in_sem.at[6]),
        pltpu.make_async_copy(cot.at[0, other], cotv.at[1, 0], in_sem.at[7]),
    ]
    for load in ends + loads:
        load.start()

    ends[0].wait()
    ends[1].wait()
    for m in range(2):
        for k in range(6):
            part = slice(k * LANE, (k + 1) * LANE)
            hs[0, m * 6 + k] = ein[0, m, :, part].astype(F32)[0:1]
            hs[1, m * 6 + k] = ein[1, m, :, part].astype(F32)[14:15]

    pl.semaphore_wait(barrier, 8)
    to_left = pltpu.make_async_remote_copy(
        src_ref=hs.at[0], dst_ref=hr.at[1], send_sem=h_send.at[0], recv_sem=h_recv.at[1],
        device_id=s_peer(S - 1), device_id_type=MESH,
    )
    to_right = pltpu.make_async_remote_copy(
        src_ref=hs.at[1], dst_ref=hr.at[0], send_sem=h_send.at[1], recv_sem=h_recv.at[0],
        device_id=s_peer(1), device_id_type=MESH,
    )
    to_left.start()
    to_right.start()
    signal(met1, beside)

    loads[0].wait()
    for m in range(2):
        for k in range(6):
            i = m * 6 + k
            xf[k] = xin[m, :, k * LANE : (k + 1) * LANE].astype(F32)
            ext[i, 7:8, :] = jnp.zeros((1, LANE), F32)
            ext[i, 8 : 8 + ROWS, :] = xf[k, pl.ds(0, ROWS, stride=2), :]
            ext[i, 8 + ROWS : 9 + ROWS, :] = jnp.zeros((1, LANE), F32)

    loads[1].wait()
    w = dwv[...].astype(F32)
    for m in range(2):
        for k in range(6):
            i = m * 6 + k
            part = slice(k * LANE, (k + 1) * LANE)
            total = w[0:1, part] * ext[i, 7 : 7 + ROWS, :]
            total = total + w[1:2, part] * ext[i, 8 : 8 + ROWS, :]
            total = total + w[2:3, part] * ext[i, 9 : 9 + ROWS, :]
            pooled[m * ROWS : (m + 1) * ROWS, part] = total.astype(BF16)
    loads[2].wait()
    for n in range(D // COL):
        cols = slice(n * COL, (n + 1) * COL)
        u = jnp.dot(pooled[...], pwv[:, cols], preferred_element_type=F32)
        enc[n] = gelu(u).astype(BF16).reshape(2, ROWS, COL)

    pl.semaphore_wait(met1, 6)
    signal(met2, [ahead, behind, z_peer(2), z_peer(Z - 2)])
    loads[6].wait()
    loads[7].wait()
    cot_copy = pltpu.make_async_remote_copy(
        src_ref=cotv.at[:, 0], dst_ref=cotv.at[:, 1], send_sem=cot_send, recv_sem=cot_recv,
        device_id=sib, device_id_type=MESH,
    )
    cot_copy.start()

    to_left.wait()
    to_right.wait()
    edge[...] = jnp.zeros_like(edge)
    for m in range(2):
        for k in range(6):
            i = m * 6 + k
            part = slice(k * LANE, (k + 1) * LANE)
            before = jnp.where(s > 0, hr[0, i], 0.0)
            after = jnp.where(s < S - 1, hr[1, i], 0.0)
            total = w[0:1, part] * before + w[1:2, part] * ext[i, 8:9, :]
            edge[2 * m : 2 * m + 1, part] = total + w[2:3, part] * ext[i, 9:10, :]
            end = 7 + ROWS
            total = w[0:1, part] * ext[i, end - 1 : end, :] + w[1:2, part] * ext[i, end : end + 1, :]
            edge[2 * m + 1 : 2 * m + 2, part] = total + w[2:3, part] * after
    edge_rows = edge[...].astype(BF16)
    row = lax.broadcasted_iota(jnp.int32, (16, COL), 0)
    for n in range(D // COL):
        cols = slice(n * COL, (n + 1) * COL)
        u = gelu(jnp.dot(edge_rows, pwv[:, cols], preferred_element_type=F32))
        for m in range(2):
            first = jnp.where(row == 0, u[2 * m : 2 * m + 1], enc[n, m, :16].astype(F32))
            enc[n, m, :16] = first.astype(BF16)
            final = jnp.where(row == 15, u[2 * m + 1 : 2 * m + 2], enc[n, m, ROWS - 16 :].astype(F32))
            enc[n, m, ROWS - 16 :] = final.astype(BF16)
        pltpu.make_async_copy(enc.at[n], enc_out.at[0, :, :, cols], enc_sem.at[n]).start()

    for load in loads[3:6]:
        load.wait()
    half = ROWS // 2

    def rows_of(micro):
        rows = jnp.concatenate([enc[n, micro] for n in range(D // COL)], axis=1)
        total = jnp.zeros((ROWS, LANE), F32)
        for n in range(D // LANE):
            wide = rows[:, n * LANE : (n + 1) * LANE].astype(F32)
            total = total + wide * wide
        return rows, lax.rsqrt(jnp.sum(total, axis=-1, keepdims=True) * (1.0 / D) + EPSILON)

    def project(micro):
        rows, scale = rows_of(micro)
        key = jnp.dot(rows, kwv[...], preferred_element_type=F32) * scale
        value = lax.dot_general(
            rows, vwv[...], (((1,), (1,)), ((), ())), preferred_element_type=F32
        )
        value = (value * scale).astype(BF16)
        kvs[micro, :ROWS] = (key * rms_of(key)).astype(BF16)
        kvs[micro, ROWS : 2 * ROWS] = value[:, :LANE]
        kvs[micro, 2 * ROWS :] = jnp.concatenate([value[:half, LANE:], value[half:, LANE:]], axis=1)
        return rows, scale

    def kv_copy(j, source, slot, device, part=slice(None)):
        return pltpu.make_async_remote_copy(
            src_ref=source.at[part], dst_ref=kvbuf.at[slot, part], send_sem=d_send.at[j],
            recv_sem=d_recv.at[j], device_id=device, device_id_type=MESH,
        )

    def relay(j, source):
        return pltpu.make_async_remote_copy(
            src_ref=source, dst_ref=kvbuf.at[2 * j + 1], send_sem=r_send.at[j],
            recv_sem=r_recv.at[j], device_id=sib, device_id_type=MESH,
        )

    parts = [pl.ds(i * 80, 80) for i in range(3)]
    to_near = [kv_copy(j, kvs.at[other], 2, near, part) for j, part in enumerate(parts)]
    forward = [kv_copy(3 + j, kvbuf.at[2], 6, behind, part) for j, part in enumerate(parts)]
    to_ahead = kv_copy(6, kvs.at[g], 4, ahead)
    project(other)
    to_near[0].start()
    to_near[1].start()
    to_near[2].start()
    rows, scale = project(g)
    relays = [relay(0, kvs.at[g])] + [relay(j, kvbuf.at[2 * j]) for j in range(1, 4)]
    relays[0].start()
    kvbuf[0] = kvs[g]

    queries = jnp.dot(rows, qwv[...], preferred_element_type=F32) * scale
    for i in range(4):
        query = queries[:, i * KEY : (i + 1) * KEY]
        q4[i] = (query * rms_of(query)).astype(BF16)
    q_copy = pltpu.make_async_remote_copy(
        src_ref=q4.at[pl.ds(2 * (1 - c), 2)], dst_ref=qall.at[:, 1], send_sem=q_send,
        recv_sem=q_recv, device_id=sib, device_id_type=MESH,
    )
    q_copy.start()
    to_ahead.start()
    qall[:, 0] = q4[pl.ds(2 * c, 2)]

    pl.semaphore_wait(met2, 4)
    signal(met3, [sib, z_peer(2), z_peer(Z - 2)])

    def turn(k):
        wide = cotv[:, :, :, k * LANE : (k + 1) * LANE].astype(F32).reshape(4 * ROWS, LANE)
        turned = jnp.transpose(wide).reshape(8, 2, S, 4 * ROWS)
        turned = jnp.where(g == 0, turned[:, 0], turned[:, 1])
        cott[k * 64 : (k + 1) * 64] = turned.reshape(64, 4 * ROWS).astype(BF16)

    cot_copy.wait()
    for j in range(3):
        to_near[j].wait_recv()
        forward[j].start()
        if j == 2:
            relays[1].start()
        for k in range(2):
            turn(2 * j + k)

    ones = jnp.ones((half, 2 * LANE - VAL), BF16)

    def group(j):
        key = kvbuf[2 * j : 2 * j + 2, :ROWS].reshape(2 * ROWS, KEY)
        head = kvbuf[2 * j : 2 * j + 2, ROWS : 2 * ROWS].reshape(2 * ROWS, LANE)
        tails = []
        for i in range(2):
            tail = kvbuf[2 * j + i, 2 * ROWS :]
            tails.append(jnp.concatenate([tail[:, : VAL - LANE], ones], axis=1))
            tails.append(jnp.concatenate([tail[:, VAL - LANE :], ones], axis=1))
        return key, jnp.concatenate([head, jnp.concatenate(tails, axis=0)], axis=1)

    def attend(query, key, value):
        scores = lax.dot_general(
            query, key, (((1,), (1,)), ((), ())), preferred_element_type=F32
        )
        weights = jnp.exp2(scores * EXP2_SCALE).astype(BF16)
        return jnp.dot(weights, value, preferred_element_type=F32)

    q_copy.wait_recv()
    relays[0].wait_recv()
    query = qall[...].reshape(4 * ROWS, KEY)
    acc[...] = attend(query, *group(0))
    to_ahead.wait_recv()
    relays[2].start()
    relays[1].wait_recv()
    acc[...] += attend(query, *group(1))
    forward[0].wait_recv()
    forward[1].wait_recv()
    forward[2].wait_recv()
    relays[3].start()
    relays[2].wait_recv()
    acc[...] += attend(query, *group(2))
    relays[3].wait_recv()
    last = group(3)

    def att_copy(t):
        return pltpu.make_async_remote_copy(
            src_ref=attx.at[t, :2], dst_ref=attx.at[t, 2:], send_sem=a_send.at[t],
            recv_sem=a_recv.at[t], device_id=partner, device_id_type=MESH,
        )

    def head(j):
        at = slice(j * 2 * ROWS, (j + 1) * 2 * ROWS)
        total = acc[at] + attend(qall[j].reshape(2 * ROWS, KEY), *last)
        inverse = 1.0 / total[:, VAL : VAL + 1]
        attended = (total[:, :VAL] * inverse).astype(BF16)
        return attended[:ROWS], attended[ROWS:]

    low = head(0)
    for i in range(2):
        attx[0, i] = low[i][:, :LANE]
    att_copy(0).start()
    high = head(1)
    for i in range(2):
        attx[1, i] = jnp.concatenate([low[i][:, LANE:], high[i][:, : 2 * LANE - VAL]], axis=1)
    att_copy(1).start()
    for i in range(2):
        attx[2, i] = high[i][:, 2 * LANE - VAL :]
    att_copy(2).start()

    def share(t, first):
        part = cott[:, : 2 * ROWS] if first else cott[:, 2 * ROWS :]
        pair = attx[t, :2] if first else attx[t, 2:]
        part = jnp.dot(part, pair.reshape(2 * ROWS, LANE), preferred_element_type=F32)
        return part.reshape(X, ROWS, LANE)

    def p1_copy(t, d):
        return pltpu.make_async_remote_copy(
            src_ref=psend.at[t, lax.rem(x + d, X)], dst_ref=p1r.at[t, d],
            send_sem=p1_send.at[t, d], recv_sem=p1_recv.at[t, d],
            device_id=x_peer(d), device_id_type=MESH,
        )

    for t in range(3):
        own[t] = share(t, True)
    for t in range(3):
        att_copy(t).wait_recv()
        full = own[t] + share(t, False)
        own[t] = full
        psend[t] = full.astype(BF16)
        for d in (2, 1, 3):
            p1_copy(t, d).start()

    def p2_copy(t, d):
        return pltpu.make_async_remote_copy(
            src_ref=p2s.at[t, lax.rem(s + d, S)], dst_ref=p2r.at[t, d],
            send_sem=p2_send.at[t, d], recv_sem=p2_recv.at[t, d],
            device_id=s_peer(d), device_id_type=MESH,
        )

    pl.semaphore_wait(met3, 3)
    for t in range(3):
        total = own[t, x]
        for d in (1, 3, 2):
            p1_copy(t, d).wait_recv()
            total = total + p1r[t, d].astype(F32)
        red1[t, : Z * S, :] = total
        red1[t, Z * S :, :] = jnp.zeros((S * 16 - Z * S, LANE), F32)
        for i in range(S):
            p2s[t, i] = red1[t, pl.ds(i, 16, stride=S), :].astype(BF16)
        for d in (4, 3, 5, 2, 6, 1, 7):
            p2_copy(t, d).start()

    for t in range(3):
        mine, theirs = p2s[t, s].astype(F32), None
        for d in (1, 7, 2, 6, 3, 5, 4):
            p2_copy(t, d).wait_recv()
            block = p2r[t, d].astype(F32)
            if d % 2 == 0:
                mine = mine + block
            else:
                theirs = block if theirs is None else theirs + block
        part = slice(t * LANE, (t + 1) * LANE)
        for i in range(Z):
            p3s[c, i, :, part] = mine[i : i + 1]
            p3s[1 - c, i, :, part] = theirs[i : i + 1]

    def p3_copy(d):
        return pltpu.make_async_remote_copy(
            src_ref=p3s.at[:, lax.rem(z + d, Z)], dst_ref=p3r.at[d], send_sem=p3_send.at[d],
            recv_sem=p3_recv.at[d], device_id=z_peer(d), device_id_type=MESH,
        )

    for d in (6, 5, 7, 4, 8, 3, 9, 2, 10, 1, 11):
        p3_copy(d).start()
    row = p3s[:, z]
    for d in (1, 11, 2, 10, 3, 9, 4, 8, 5, 7, 6):
        p3_copy(d).wait_recv()
        row = row + p3r[d]
    row = row * norm
    grad_out[:, : 2 * VAL] = row[0]
    grad_out[:, 2 * VAL :] = row[1]

    cols = pl.ds(0, COL)
    for n in range(D // COL):
        pltpu.make_async_copy(enc.at[n], enc_out.at[0, :, :, cols], enc_sem.at[n]).wait()
    for copy in to_near + forward + [to_ahead] + relays + [q_copy]:
        copy.wait_send()
    for t in range(3):
        att_copy(t).wait_send()
        for d in range(1, X):
            p1_copy(t, d).wait_send()
        for d in range(1, S):
            p2_copy(t, d).wait_send()
    for d in range(1, Z):
        p3_copy(d).wait_send()


def deliver(encoded, grad, encoded_out, grad_out, rows, line, load_sem, store_sem):
    half = ROWS // 2
    places = []
    for i in range(4):
        at = (i // 2, pl.ds(i % 2 * half, half))
        places.append((encoded.at[0, *at], rows.at[at], encoded_out.at[0, *at]))
    places.append((grad, line, grad_out))
    loads = [
        pltpu.make_async_copy(source, held, load_sem.at[i])
        for i, (source, held, _) in enumerate(places)
    ]
    stores = [
        pltpu.make_async_copy(held, target, store_sem.at[i])
        for i, (_, held, target) in enumerate(places)
    ]
    for load in loads:
        load.start()
    for load, store in zip(loads, stores):
        load.wait()
        store.start()
    for store in stores:
        store.wait()


def per_device(dna, dw, pw, qw, kw, vw, cot):
    norm = 1.0 / math.sqrt(X * Z * dna.shape[1])
    dma = pltpu.SemaphoreType.DMA
    vmem = pltpu.VMEM
    hbm = pl.BlockSpec(memory_space=pltpu.MemorySpace.HBM)
    encoded, grad = pl.pallas_call(
        functools.partial(kernel, norm),
        out_shape=(
            jax.ShapeDtypeStruct((1, 2, ROWS, D), BF16),
            jax.ShapeDtypeStruct((1, 4 * VAL), F32),
        ),
        in_specs=[hbm] * 7,
        out_specs=(hbm, pl.BlockSpec(memory_space=pltpu.VMEM)),
        scratch_shapes=[
            vmem((2, 2, 16, C_IN), BF16),
            vmem((2, 2 * ROWS, C_IN), BF16),
            vmem((3, C_IN), BF16),
            vmem((C_IN, D), BF16),
            vmem((D, 4 * KEY), BF16),
            vmem((D, KEY), BF16),
            vmem((VAL, D), BF16),
            vmem((2, 2, ROWS, C_IN), BF16),
            vmem((6, 2 * ROWS, LANE), F32),
            vmem((12, ROWS + 16, LANE), F32),
            vmem((2 * ROWS, C_IN), BF16),
            vmem((16, C_IN), F32),
            vmem((D // COL, 2, ROWS, COL), BF16),
            vmem((2, 12, 1, LANE), F32),
            vmem((2, 12, 1, LANE), F32),
            vmem((4, ROWS, KEY), BF16),
            vmem((2, 2, ROWS, KEY), BF16),
            vmem((2, KV_ROWS, LANE), BF16),
            vmem((8, KV_ROWS, LANE), BF16),
            vmem((4 * ROWS, 2 * LANE), F32),
            vmem((X * ROWS, 4 * ROWS), BF16),
            vmem((3, 4, ROWS, LANE), BF16),
            vmem((3, X, ROWS, LANE), F32),
            vmem((3, X, ROWS, LANE), BF16),
            vmem((3, X, ROWS, LANE), BF16),
            vmem((3, 16 * S, LANE), F32),
            vmem((3, S, 16, LANE), BF16),
            vmem((3, S, 16, LANE), BF16),
            vmem((2, Z, 1, 2 * VAL), F32),
            vmem((Z, 2, 1, 2 * VAL), F32),
            dma((10,)), dma((D // COL,)), dma((2,)), dma((2,)), dma, dma, dma, dma,
            dma((7,)), dma((7,)), dma((4,)), dma((4,)), dma((3,)), dma((3,)),
            dma((3, X)), dma((3, X)), dma((3, S)), dma((3, S)), dma((Z,)), dma((Z,)),
            pltpu.SemaphoreType.REGULAR, pltpu.SemaphoreType.REGULAR, pltpu.SemaphoreType.REGULAR,
        ],
        compiler_params=pltpu.CompilerParams(
            collective_id=0, has_side_effects=True, vmem_limit_bytes=62 * 2**20
        ),
        name="window_step",
    )(dna, dw, pw, qw, kw, vw.T, cot)
    return pl.pallas_call(
        deliver,
        out_shape=(
            jax.ShapeDtypeStruct(encoded.shape, BF16),
            jax.ShapeDtypeStruct(grad.shape, F32),
        ),
        in_specs=[hbm] * 2,
        out_specs=(hbm, hbm),
        scratch_shapes=[
            vmem((2, ROWS, D), BF16), vmem((1, 4 * VAL), F32), dma((5,)), dma((5,)),
        ],
        compiler_params=pltpu.CompilerParams(vmem_limit_bytes=62 * 2**20),
        name="deliver",
    )(encoded, grad)


def solution(mesh):
    rows = P("batch", None, "seq", None)
    return jax.shard_map(
        per_device,
        mesh=mesh,
        in_specs=(rows, P(), P(), P(), P(), P(), rows),
        out_specs=(rows, P(("batch", "segment", "seq"), None)),
        check_vma=False,
    )
```

```python
import functools
import math

import jax
import jax.numpy as jnp
from jax import lax
from jax.experimental import pallas as pl
from jax.experimental.pallas import tpu as pltpu
from jax.sharding import PartitionSpec as P

MESH = pl.DeviceIdType.MESH
F32 = jnp.float32
BF16 = jnp.bfloat16

C_IN = 768
D = 1536
KEY = 128
VAL = 192
ROWS = 96
X, Z, S = 4, 12, 8
EPSILON = 1e-06
LANE = 128
COL = 256
KV_ROWS = 2 * ROWS + ROWS // 2
EXP2_SCALE = math.log2(math.e) / math.sqrt(KEY)


def gelu(u):
    inner = math.sqrt(2.0 / math.pi) * (u + 0.044715 * (u * u * u))
    return 0.5 * u * (1.0 + jnp.tanh(inner))


def rms_of(values):
    return lax.rsqrt(jnp.mean(values * values, axis=-1, keepdims=True) + EPSILON)


def kernel(
    norm,
    dna, dw, pw, qw, kw, vw, cot,
    enc_out, grad_out,
    ein, xin, dwv, pwv, qwv, kwv, vwv, cotv,
    xf, ext, pooled, edge, enc,
    hs, hr, q4, qall, kvs, kvbuf, acc, cott, attx, own, psend, p1r, red1, p2s, p2r, p3s, p3r,
    in_sem, enc_sem, h_send, h_recv, cot_send, cot_recv, q_send, q_recv,
    d_send, d_recv, r_send, r_recv, a_send, a_recv,
    p1_send, p1_recv, p2_send, p2_recv, p3_send, p3_recv, met1, met2, met3,
):
    b, g, s = lax.axis_index("batch"), lax.axis_index("segment"), lax.axis_index("seq")
    x, z = b // Z, lax.rem(b, Z)
    h, c = s // 2, lax.rem(s, 2)
    other = 1 - g
    sign = 2 * g - 1

    def x_peer(d):
        return (lax.rem(x + d, X) * Z + z, g, s)

    def s_peer(d):
        return (b, g, lax.rem(s + d, S))

    def z_peer(d):
        return (x * Z + lax.rem(z + d, Z), g, s)

    sib = (b, g, h * 2 + (1 - c))
    partner = (b, other, s)
    near = (b, other, lax.rem(h + sign + 4, 4) * 2 + c)
    ahead = (b, g, lax.rem(h + sign + 4, 4) * 2 + c)
    behind = (b, g, lax.rem(h - sign + 4, 4) * 2 + c)
    cross = (b, g, lax.rem(s + 2 * c - 1 + S, S))

    def signal(semaphore, devices):
        for device in devices:
            pl.semaphore_signal(semaphore, inc=1, device_id=device, device_id_type=MESH)

    barrier = pltpu.get_barrier_semaphore()
    beside = [partner, near, x_peer(1), x_peer(X - 1), z_peer(1), z_peer(Z - 1)]
    signal(barrier, [cross, sib] + beside)

    ends = [
        pltpu.make_async_copy(dna.at[0, :, pl.ds(0, 16)], ein.at[0], in_sem.at[8]),
        pltpu.make_async_copy(dna.at[0, :, pl.ds(2 * ROWS - 16, 16)], ein.at[1], in_sem.at[9]),
    ]
    loads = [
        pltpu.make_async_copy(dna.at[0], xin, in_sem.at[0]),
        pltpu.make_async_copy(dw, dwv, in_sem.at[1]),
        pltpu.make_async_copy(pw, pwv, in_sem.at[2]),
        pltpu.make_async_copy(kw, kwv, in_sem.at[3]),
        pltpu.make_async_copy(vw, vwv, in_sem.at[4]),
        pltpu.make_async_copy(qw, qwv, in_sem.at[5]),
        pltpu.make_async_copy(cot.at[0, g], cotv.at[0, 0], in_sem.at[6]),
        pltpu.make_async_copy(cot.at[0, other], cotv.at[1, 0], in_sem.at[7]),
    ]
    for load in ends + loads:
        load.start()

    ends[0].wait()
    ends[1].wait()
    for m in range(2):
        for k in range(6):
            part = slice(k * LANE, (k + 1) * LANE)
            hs[0, m * 6 + k] = ein[0, m, :, part].astype(F32)[0:1]
            hs[1, m * 6 + k] = ein[1, m, :, part].astype(F32)[14:15]

    pl.semaphore_wait(barrier, 8)
    to_left = pltpu.make_async_remote_copy(
        src_ref=hs.at[0], dst_ref=hr.at[1], send_sem=h_send.at[0], recv_sem=h_recv.at[1],
        device_id=s_peer(S - 1), device_id_type=MESH,
    )
    to_right = pltpu.make_async_remote_copy(
        src_ref=hs.at[1], dst_ref=hr.at[0], send_sem=h_send.at[1], recv_sem=h_recv.at[0],
        device_id=s_peer(1), device_id_type=MESH,
    )
    to_left.start()
    to_right.start()
    signal(met1, beside)

    loads[0].wait()
    for m in range(2):
        for k in range(6):
            i = m * 6 + k
            xf[k] = xin[m, :, k * LANE : (k + 1) * LANE].astype(F32)
            ext[i, 7:8, :] = jnp.zeros((1, LANE), F32)
            ext[i, 8 : 8 + ROWS, :] = xf[k, pl.ds(0, ROWS, stride=2), :]
            ext[i, 8 + ROWS : 9 + ROWS, :] = jnp.zeros((1, LANE), F32)

    loads[1].wait()
    w = dwv[...].astype(F32)
    for m in range(2):
        for k in range(6):
            i = m * 6 + k
            part = slice(k * LANE, (k + 1) * LANE)
            total = w[0:1, part] * ext[i, 7 : 7 + ROWS, :]
            total = total + w[1:2, part] * ext[i, 8 : 8 + ROWS, :]
            total = total + w[2:3, part] * ext[i, 9 : 9 + ROWS, :]
            pooled[m * ROWS : (m + 1) * ROWS, part] = total.astype(BF16)
    loads[2].wait()
    for n in range(D // COL):
        cols = slice(n * COL, (n + 1) * COL)
        u = jnp.dot(pooled[...], pwv[:, cols], preferred_element_type=F32)
        enc[n] = gelu(u).astype(BF16).reshape(2, ROWS, COL)

    loads[6].wait()
    loads[7].wait()
    cot_copy = pltpu.make_async_remote_copy(
        src_ref=cotv.at[:, 0], dst_ref=cotv.at[:, 1], send_sem=cot_send, recv_sem=cot_recv,
        device_id=sib, device_id_type=MESH,
    )
    cot_copy.start()

    to_left.wait_recv()
    to_right.wait_recv()
    edge[...] = jnp.zeros_like(edge)
    for m in range(2):
        for k in range(6):
            i = m * 6 + k
            part = slice(k * LANE, (k + 1) * LANE)
            before = jnp.where(s > 0, hr[0, i], 0.0)
            after = jnp.where(s < S - 1, hr[1, i], 0.0)
            total = w[0:1, part] * before + w[1:2, part] * ext[i, 8:9, :]
            edge[2 * m : 2 * m + 1, part] = total + w[2:3, part] * ext[i, 9:10, :]
            end = 7 + ROWS
            total = w[0:1, part] * ext[i, end - 1 : end, :] + w[1:2, part] * ext[i, end : end + 1, :]
            edge[2 * m + 1 : 2 * m + 2, part] = total + w[2:3, part] * after
    edge_rows = edge[...].astype(BF16)
    row = lax.broadcasted_iota(jnp.int32, (16, COL), 0)
    for n in range(D // COL):
        cols = slice(n * COL, (n + 1) * COL)
        u = gelu(jnp.dot(edge_rows, pwv[:, cols], preferred_element_type=F32))
        for m in range(2):
            first = jnp.where(row == 0, u[2 * m : 2 * m + 1], enc[n, m, :16].astype(F32))
            enc[n, m, :16] = first.astype(BF16)
            final = jnp.where(row == 15, u[2 * m + 1 : 2 * m + 2], enc[n, m, ROWS - 16 :].astype(F32))
            enc[n, m, ROWS - 16 :] = final.astype(BF16)
        pltpu.make_async_copy(enc.at[n], enc_out.at[0, :, :, cols], enc_sem.at[n]).start()

    for load in loads[3:6]:
        load.wait()
    half = ROWS // 2

    def rows_of(micro):
        rows = jnp.concatenate([enc[n, micro] for n in range(D // COL)], axis=1)
        total = jnp.zeros((ROWS, LANE), F32)
        for n in range(D // LANE):
            wide = rows[:, n * LANE : (n + 1) * LANE].astype(F32)
            total = total + wide * wide
        return rows, lax.rsqrt(jnp.sum(total, axis=-1, keepdims=True) * (1.0 / D) + EPSILON)

    def project(micro):
        rows, scale = rows_of(micro)
        key = jnp.dot(rows, kwv[...], preferred_element_type=F32) * scale
        value = lax.dot_general(
            rows, vwv[...], (((1,), (1,)), ((), ())), preferred_element_type=F32
        )
        value = (value * scale).astype(BF16)
        kvs[micro, :ROWS] = (key * rms_of(key)).astype(BF16)
        kvs[micro, ROWS : 2 * ROWS] = value[:, :LANE]
        kvs[micro, 2 * ROWS :] = jnp.concatenate([value[:half, LANE:], value[half:, LANE:]], axis=1)
        return rows, scale

    def kv_copy(j, source, slot, device, part=slice(None)):
        return pltpu.make_async_remote_copy(
            src_ref=source.at[part], dst_ref=kvbuf.at[slot, part], send_sem=d_send.at[j],
            recv_sem=d_recv.at[j], device_id=device, device_id_type=MESH,
        )

    def relay(j, source):
        return pltpu.make_async_remote_copy(
            src_ref=source, dst_ref=kvbuf.at[2 * j + 1], send_sem=r_send.at[j],
            recv_sem=r_recv.at[j], device_id=sib, device_id_type=MESH,
        )

    parts = [pl.ds(i * 80, 80) for i in range(3)]
    to_near = [kv_copy(j, kvs.at[other], 2, near, part) for j, part in enumerate(parts)]
    forward = [kv_copy(3 + j, kvbuf.at[2], 6, behind, part) for j, part in enumerate(parts)]
    to_ahead = kv_copy(6, kvs.at[g], 4, ahead)
    project(other)
    to_near[0].start()
    to_near[1].start()
    to_near[2].start()
    pl.semaphore_wait(met1, 6)
    signal(met2, [ahead, behind, z_peer(2), z_peer(Z - 2)])
    rows, scale = project(g)
    relays = [relay(0, kvs.at[g])] + [relay(j, kvbuf.at[2 * j]) for j in range(1, 4)]
    relays[0].start()
    kvbuf[0] = kvs[g]

    queries = jnp.dot(rows, qwv[...], preferred_element_type=F32) * scale
    for i in range(4):
        query = queries[:, i * KEY : (i + 1) * KEY]
        q4[i] = (query * rms_of(query)).astype(BF16)
    q_copy = pltpu.make_async_remote_copy(
        src_ref=q4.at[pl.ds(2 * (1 - c), 2)], dst_ref=qall.at[:, 1], send_sem=q_send,
        recv_sem=q_recv, device_id=sib, device_id_type=MESH,
    )
    q_copy.start()
    to_ahead.start()
    qall[:, 0] = q4[pl.ds(2 * c, 2)]


    def turn(k):
        wide = cotv[:, :, :, k * LANE : (k + 1) * LANE].astype(F32).reshape(4 * ROWS, LANE)
        turned = jnp.transpose(wide).reshape(8, 2, S, 4 * ROWS)
        turned = jnp.where(g == 0, turned[:, 0], turned[:, 1])
        cott[k * 64 : (k + 1) * 64] = turned.reshape(64, 4 * ROWS).astype(BF16)

    cot_copy.wait()
    for j in range(3):
        to_near[j].wait_recv()
        forward[j].start()
        if j == 2:
            relays[1].start()
        for k in range(2):
            turn(2 * j + k)

    ones = jnp.ones((half, 2 * LANE - VAL), BF16)

    def group(j):
        key = kvbuf[2 * j : 2 * j + 2, :ROWS].reshape(2 * ROWS, KEY)
        head = kvbuf[2 * j : 2 * j + 2, ROWS : 2 * ROWS].reshape(2 * ROWS, LANE)
        tails = []
        for i in range(2):
            tail = kvbuf[2 * j + i, 2 * ROWS :]
            tails.append(jnp.concatenate([tail[:, : VAL - LANE], ones], axis=1))
            tails.append(jnp.concatenate([tail[:, VAL - LANE :], ones], axis=1))
        return key, jnp.concatenate([head, jnp.concatenate(tails, axis=0)], axis=1)

    def attend(query, key, value):
        scores = lax.dot_general(
            query, key, (((1,), (1,)), ((), ())), preferred_element_type=F32
        )
        weights = jnp.exp2(scores * EXP2_SCALE).astype(BF16)
        return jnp.dot(weights, value, preferred_element_type=F32)

    pl.semaphore_wait(met2, 4)
    signal(met3, [sib, z_peer(2), z_peer(Z - 2)])
    q_copy.wait_recv()
    relays[0].wait_recv()
    query = qall[...].reshape(4 * ROWS, KEY)
    acc[...] = attend(query, *group(0))
    to_ahead.wait_recv()
    relays[2].start()
    relays[1].wait_recv()
    acc[...] += attend(query, *group(1))
    forward[0].wait_recv()
    forward[1].wait_recv()
    forward[2].wait_recv()
    relays[3].start()
    relays[2].wait_recv()
    acc[...] += attend(query, *group(2))
    relays[3].wait_recv()
    last = group(3)

    def att_copy(t):
        return pltpu.make_async_remote_copy(
            src_ref=attx.at[t, :2], dst_ref=attx.at[t, 2:], send_sem=a_send.at[t],
            recv_sem=a_recv.at[t], device_id=partner, device_id_type=MESH,
        )

    def head(j):
        at = slice(j * 2 * ROWS, (j + 1) * 2 * ROWS)
        total = acc[at] + attend(qall[j].reshape(2 * ROWS, KEY), *last)
        inverse = 1.0 / total[:, VAL : VAL + 1]
        attended = (total[:, :VAL] * inverse).astype(BF16)
        return attended[:ROWS], attended[ROWS:]

    low = head(0)
    for i in range(2):
        attx[0, i] = low[i][:, :LANE]
    att_copy(0).start()
    high = head(1)
    for i in range(2):
        attx[1, i] = jnp.concatenate([low[i][:, LANE:], high[i][:, : 2 * LANE - VAL]], axis=1)
    att_copy(1).start()
    for i in range(2):
        attx[2, i] = high[i][:, 2 * LANE - VAL :]
    att_copy(2).start()

    def share(t, first):
        part = cott[:, : 2 * ROWS] if first else cott[:, 2 * ROWS :]
        pair = attx[t, :2] if first else attx[t, 2:]
        part = jnp.dot(part, pair.reshape(2 * ROWS, LANE), preferred_element_type=F32)
        return part.reshape(X, ROWS, LANE)

    def p1_copy(t, d):
        return pltpu.make_async_remote_copy(
            src_ref=psend.at[t, lax.rem(x + d, X)], dst_ref=p1r.at[t, d],
            send_sem=p1_send.at[t, d], recv_sem=p1_recv.at[t, d],
            device_id=x_peer(d), device_id_type=MESH,
        )

    for t in range(3):
        own[t] = share(t, True)
        red1[t, Z * S :, :] = jnp.zeros((S * 16 - Z * S, LANE), F32)
    for t in range(3):
        att_copy(t).wait_recv()
        full = own[t] + share(t, False)
        own[t] = full
        psend[t] = full.astype(BF16)
        for d in (2, 1, 3):
            p1_copy(t, d).start()

    def p2_copy(t, d):
        return pltpu.make_async_remote_copy(
            src_ref=p2s.at[t, lax.rem(s + d, S)], dst_ref=p2r.at[t, d],
            send_sem=p2_send.at[t, d], recv_sem=p2_recv.at[t, d],
            device_id=s_peer(d), device_id_type=MESH,
        )

    pl.semaphore_wait(met3, 3)
    for t in range(3):
        total = own[t, x]
        for d in (1, 3, 2):
            p1_copy(t, d).wait_recv()
            total = total + p1r[t, d].astype(F32)
        red1[t, : Z * S, :] = total
        for i in range(S):
            p2s[t, i] = red1[t, pl.ds(i, 16, stride=S), :].astype(BF16)
        for d in (4, 3, 5, 2, 6, 1, 7):
            p2_copy(t, d).start()

    for t in range(3):
        mine, theirs = p2s[t, s].astype(F32), None
        for d in (1, 7, 2, 6, 3, 5, 4):
            p2_copy(t, d).wait_recv()
            block = p2r[t, d].astype(F32)
            if d % 2 == 0:
                mine = mine + block
            else:
                theirs = block if theirs is None else theirs + block
        part = slice(t * LANE, (t + 1) * LANE)
        for i in range(Z):
            p3s[c, i, :, part] = mine[i : i + 1]
            p3s[1 - c, i, :, part] = theirs[i : i + 1]

    def p3_copy(d):
        return pltpu.make_async_remote_copy(
            src_ref=p3s.at[:, lax.rem(z + d, Z)], dst_ref=p3r.at[d], send_sem=p3_send.at[d],
            recv_sem=p3_recv.at[d], device_id=z_peer(d), device_id_type=MESH,
        )

    for d in (6, 5, 7, 4, 8, 3, 9, 2, 10, 1, 11):
        p3_copy(d).start()
    row = p3s[:, z]
    for d in (1, 11, 2, 10, 3, 9, 4, 8, 5, 7, 6):
        p3_copy(d).wait_recv()
        row = row + p3r[d]
    row = row * norm
    grad_out[:, : 2 * VAL] = row[0]
    grad_out[:, 2 * VAL :] = row[1]

    to_left.wait_send()
    to_right.wait_send()
    cols = pl.ds(0, COL)
    for n in range(D // COL):
        pltpu.make_async_copy(enc.at[n], enc_out.at[0, :, :, cols], enc_sem.at[n]).wait()
    for copy in to_near + forward + [to_ahead] + relays + [q_copy]:
        copy.wait_send()
    for t in range(3):
        att_copy(t).wait_send()
        for d in range(1, X):
            p1_copy(t, d).wait_send()
        for d in range(1, S):
            p2_copy(t, d).wait_send()
    for d in range(1, Z):
        p3_copy(d).wait_send()


def deliver(encoded, grad, encoded_out, grad_out, rows, line, load_sem, store_sem):
    half = ROWS // 2
    places = []
    for i in range(4):
        at = (i // 2, pl.ds(i % 2 * half, half))
        places.append((encoded.at[0, *at], rows.at[at], encoded_out.at[0, *at]))
    places.append((grad, line, grad_out))
    loads = [
        pltpu.make_async_copy(source, held, load_sem.at[i])
        for i, (source, held, _) in enumerate(places)
    ]
    stores = [
        pltpu.make_async_copy(held, target, store_sem.at[i])
        for i, (_, held, target) in enumerate(places)
    ]
    for load in loads:
        load.start()
    for load, store in zip(loads, stores):
        load.wait()
        store.start()
    for store in stores:
        store.wait()


def per_device(dna, dw, pw, qw, kw, vw, cot):
    norm = 1.0 / math.sqrt(X * Z * dna.shape[1])
    dma = pltpu.SemaphoreType.DMA
    vmem = pltpu.VMEM
    hbm = pl.BlockSpec(memory_space=pltpu.MemorySpace.HBM)
    encoded, grad = pl.pallas_call(
        functools.partial(kernel, norm),
        out_shape=(
            jax.ShapeDtypeStruct((1, 2, ROWS, D), BF16),
            jax.ShapeDtypeStruct((1, 4 * VAL), F32),
        ),
        in_specs=[hbm] * 7,
        out_specs=(hbm, pl.BlockSpec(memory_space=pltpu.VMEM)),
        scratch_shapes=[
            vmem((2, 2, 16, C_IN), BF16),
            vmem((2, 2 * ROWS, C_IN), BF16),
            vmem((3, C_IN), BF16),
            vmem((C_IN, D), BF16),
            vmem((D, 4 * KEY), BF16),
            vmem((D, KEY), BF16),
            vmem((VAL, D), BF16),
            vmem((2, 2, ROWS, C_IN), BF16),
            vmem((6, 2 * ROWS, LANE), F32),
            vmem((12, ROWS + 16, LANE), F32),
            vmem((2 * ROWS, C_IN), BF16),
            vmem((16, C_IN), F32),
            vmem((D // COL, 2, ROWS, COL), BF16),
            vmem((2, 12, 1, LANE), F32),
            vmem((2, 12, 1, LANE), F32),
            vmem((4, ROWS, KEY), BF16),
            vmem((2, 2, ROWS, KEY), BF16),
            vmem((2, KV_ROWS, LANE), BF16),
            vmem((8, KV_ROWS, LANE), BF16),
            vmem((4 * ROWS, 2 * LANE), F32),
            vmem((X * ROWS, 4 * ROWS), BF16),
            vmem((3, 4, ROWS, LANE), BF16),
            vmem((3, X, ROWS, LANE), F32),
            vmem((3, X, ROWS, LANE), BF16),
            vmem((3, X, ROWS, LANE), BF16),
            vmem((3, 16 * S, LANE), F32),
            vmem((3, S, 16, LANE), BF16),
            vmem((3, S, 16, LANE), BF16),
            vmem((2, Z, 1, 2 * VAL), F32),
            vmem((Z, 2, 1, 2 * VAL), F32),
            dma((10,)), dma((D // COL,)), dma((2,)), dma((2,)), dma, dma, dma, dma,
            dma((7,)), dma((7,)), dma((4,)), dma((4,)), dma((3,)), dma((3,)),
            dma((3, X)), dma((3, X)), dma((3, S)), dma((3, S)), dma((Z,)), dma((Z,)),
            pltpu.SemaphoreType.REGULAR, pltpu.SemaphoreType.REGULAR, pltpu.SemaphoreType.REGULAR,
        ],
        compiler_params=pltpu.CompilerParams(
            collective_id=0, has_side_effects=True, vmem_limit_bytes=62 * 2**20
        ),
        name="window_step",
    )(dna, dw, pw, qw, kw, vw.T, cot)
    return pl.pallas_call(
        deliver,
        out_shape=(
            jax.ShapeDtypeStruct(encoded.shape, BF16),
            jax.ShapeDtypeStruct(grad.shape, F32),
        ),
        in_specs=[hbm] * 2,
        out_specs=(hbm, hbm),
        scratch_shapes=[
            vmem((2, ROWS, D), BF16), vmem((1, 4 * VAL), F32), dma((5,)), dma((5,)),
        ],
        compiler_params=pltpu.CompilerParams(vmem_limit_bytes=62 * 2**20),
        name="deliver",
    )(encoded, grad)


def solution(mesh):
    rows = P("batch", None, "seq", None)
    return jax.shard_map(
        per_device,
        mesh=mesh,
        in_specs=(rows, P(), P(), P(), P(), P(), rows),
        out_specs=(rows, P(("batch", "segment", "seq"), None)),
        check_vma=False,
    )
```
